512 devices in a mesh: role: 4 (over x), ep: 64 (over z, y), dp: 2 (over core).
Axes of the slice: x: 4, y: 8, z: 8, core: 2. Of those that a mesh axis runs over, the one named last changes fastest.
Arguments:
- latents: bfloat16 [16, 4096, 1536], P(('role', 'dp'), 'ep'), may hold values from -6 to 6
- noise: bfloat16 [1, 16, 4096, 1536], P(None, ('role', 'dp'), 'ep'), may hold values from -6 to 6
- expert_ids: int32 [1, 16, 4096, 6], P(None, ('role', 'dp'), 'ep'), may hold values from 0 to 63, all different within a row; in each aligned block of 64 rows (0 to 63, 64 to 127, ..., all dimensions but the last counted through in order) at most 7 rows name the same one
- gate_values: float32 [1, 16, 4096, 6], P(None, ('role', 'dp'), 'ep'), may hold values from 0.1 to 1
- advantages: float32 [16], P(('role', 'dp')), may hold values from -4 to 4
- expert_pair: bfloat16 [64, 2, 768, 1536], P('ep', None, ('role', 'dp')), may hold values from -6 to 6
Outputs:
- final_latents: bfloat16 [16, 4096, 1536], P(('role', 'dp'), 'ep')
- new_down: bfloat16 [64, 768, 1536], P('ep')
The draws below stay inside these ranges and needn't reach their ends.
Inputs may be any that keep to these rules, and one draw needn't show every extreme that they name: `expert_ids`: each row names 6 different experts. In every aligned block of 64 rows (steps, images and tokens taken together in order; one index of ep holds one block of an image at a step) no expert is named more than 7 times, a bound that some block reaches.
All inputs are finite; a program needn't handle non-finite values.
Results may differ from the reference program's by a relative error of at most 0.008.
Values may be sent and summed in bfloat16 or wider, within the bound.
A program may use at most 128 MiB of HBM per device.

```python
import math
import jax
import jax.numpy as jnp
import numpy as np
from jax import lax

D = 1536
HID = 768
EXPERTS = 64
TOP = 6
STEPS = 1
TOK_DEV = 64
IMG_DEV = 2
CAP = 7
IMG_TOK = 4096
IMAGES = 16
N_EP = 64


def levels(key, shape, pieces, low, largest):
    def one(dim, parts):
        heights = jax.random.uniform(jax.random.fold_in(jax.random.fold_in(key, 6), dim), (parts,), jnp.float32, low / len(pieces), largest / len(pieces))
        return jnp.repeat(jnp.exp(heights), shape[dim] // parts).reshape((-1,) + (1,) * (len(shape) - dim - 1))

    gain = one(*pieces[0])
    for cut in pieces[1:]:
        gain = gain * one(*cut)
    return gain


def shared_out(key, own, number, rows, number_of, top, bound, lean):
    ranking = jax.random.permutation(key, number_of)
    heavy_load, common = shares(number_of, rows * top, bound, lean, True), shares(number_of, rows * top, bound, lean, False)
    places = jnp.arange(number_of)

    def named(lengths, offset_by):
        used = int((lengths > 0).sum())
        fixed = max(1, used // 4)
        passed = fixed + (places - fixed + offset_by * (used - fixed)) % max(1, number_of - fixed)
        return jnp.zeros((number_of,), jnp.int32).at[ranking[jnp.where(places < fixed, places, passed)]].set(jnp.asarray(lengths, jnp.int32))

    lengths = jnp.where(number % 4 == 0, named(heavy_load, number // 4), named(common, number - number // 4 - 1))
    mixed = jax.random.permutation(jax.random.fold_in(own, 3), number_of)
    source_of, sink = mixed[0:number_of // 2 * 2:2], mixed[1:number_of // 2 * 2:2]
    room = jnp.minimum(lengths[source_of] - 1, bound - lengths[sink]) // 2
    room = jnp.where((source_of == ranking[0]) | (sink == ranking[0]) | (lengths[sink] == 0), 0, jnp.maximum(room, 0))
    passed = jax.random.randint(jax.random.fold_in(own, 4), (number_of // 2,), 0, 1 << 20) % (room + 1)
    lengths = lengths.at[source_of].add(-passed).at[sink].add(passed)
    members = jnp.searchsorted(jnp.cumsum(lengths), jnp.arange(rows * top), side="right").astype(jnp.int32)
    grid = members.reshape(top, rows).T
    grid = grid[jax.random.permutation(jax.random.fold_in(own, 1), rows)]
    offset_by = jax.random.randint(jax.random.fold_in(own, 2), (rows, 1), 0, top)
    return jnp.take_along_axis(grid, (jnp.arange(top)[None, :] + offset_by) % top, axis=1)


def shares(count, total, limit, slope, full):
    weights = [(1 << 20) // math.isqrt(rank ** slope) + 1 for rank in range(1, count + 1)]
    largest = limit if full else min(limit, max(-(-total // count), total * weights[0] // sum(weights)))
    least = 1 if total - largest >= count - 1 else 0
    holding, rest = [largest] + [least] * (count - 1), total - largest - least * (count - 1)
    while rest > 0:
        movable = [i for i in range(1, count) if holding[i] < largest] or [i for i in range(1, count) if holding[i] < limit]
        whole, budget = sum([weights[i] for i in movable]), rest
        for i in movable:
            addition = min(limit - holding[i], max(1, budget * weights[i] // whole), rest)
            holding[i] = holding[i] + addition
            rest = rest - addition
    return np.array(holding)


def gaussian(stream_key, extent, deviation, bound, pieces=(), kind=jnp.bfloat16):
    values = deviation * jax.random.normal(stream_key, extent, jnp.float32)
    if pieces:
        values = values * levels(stream_key, extent, pieces, -0.22, 0.18)
    return jnp.clip(values, -bound, bound).astype(kind)


def setup_inputs(seed: int = 0) -> dict:
    keys = jax.random.split(jax.random.key(seed), 7)
    latents = gaussian(keys[0], (IMAGES, IMG_TOK, D), 1.0, 6.0, ((0, 8), (1, 64)))
    noise = gaussian(keys[1], (STEPS, IMAGES, IMG_TOK, D), 1.0, 6.0, ((1, 8), (2, 64)))
    expert_ids_keys = jax.random.split(jax.random.fold_in(keys[2], 1), STEPS * IMAGES * IMG_TOK // TOK_DEV)
    expert_ids_turns = jax.random.permutation(jax.random.fold_in(keys[2], 3), STEPS * IMAGES * IMG_TOK // TOK_DEV)
    expert_ids = jax.vmap(lambda own, number: shared_out(jax.random.fold_in(keys[2], 2), own, number, TOK_DEV, EXPERTS, TOP, CAP, 2))(expert_ids_keys, expert_ids_turns).reshape((STEPS, IMAGES, IMG_TOK, TOP))
    gate_values = jnp.clip(jnp.exp(math.log(1.0) - 2.3025851 * jax.random.uniform(keys[3], (STEPS, IMAGES, IMG_TOK, TOP), jnp.float32) ** levels(keys[3], (STEPS, IMAGES, IMG_TOK, TOP), ((1, 8), (2, 64)), -0.2, 0.2)), 0.1, 1.0)
    advantages = gaussian(keys[4], (IMAGES,), 1.0, 4.0, ((0, 8),), jnp.float32)
    expert_pair = gaussian(keys[5], (EXPERTS, 2, HID, D), 1.0, 6.0, ((0, 64), (2, 8)))
    return dict(latents=latents, noise=noise, expert_ids=expert_ids, gate_values=gate_values, advantages=advantages, expert_pair=expert_pair)


def coefficients(section):
    moment = 0.95 - 0.4 * section
    noise_level = 0.3 * math.sqrt(moment / (1.0 - moment))
    factor = noise_level * noise_level / (2.0 * moment)
    keep_gain = 1.0 - 0.4 * factor
    drift_gain = -0.4 * (1.0 + factor * (1.0 - moment))
    noise_gain = noise_level * math.sqrt(0.4)
    return (keep_gain, drift_gain, noise_gain)

def slot_tables(picked, weights):
    images = picked.shape[0]
    blocks = picked.reshape(images, N_EP, TOK_DEV * TOP).astype(jnp.int32)
    onehot = (blocks[..., None] == jnp.arange(EXPERTS, dtype=jnp.int32)).astype(jnp.int32)
    ranks = jnp.cumsum(onehot, axis=2).astype(jnp.int32) - 1
    placed = lax.optimization_barrier(jnp.sum(ranks * onehot, axis=3)).astype(jnp.int32)
    source = jnp.arange(N_EP, dtype=jnp.int32)[None, :, None]
    column = jnp.broadcast_to(source * CAP + placed, blocks.shape).astype(jnp.int32)
    token_pos = (jnp.arange(TOK_DEV * TOP, dtype=jnp.int32) // TOP)[None, None, :]
    token_ids = jnp.broadcast_to(source * TOK_DEV + token_pos, blocks.shape).astype(jnp.int32)
    image_ids = jnp.broadcast_to(jnp.arange(images, dtype=jnp.int32)[:, None, None], blocks.shape)
    table_token = jnp.full((images, EXPERTS, N_EP * CAP), IMG_TOK, jnp.int32)
    table_token = table_token.at[image_ids, blocks, column].set(token_ids)
    table_gate = jnp.zeros((images, EXPERTS, N_EP * CAP), jnp.float32)
    table_gate = table_gate.at[image_ids, blocks, column].set(weights.reshape(blocks.shape))
    return (jnp.transpose(table_token, (1, 0, 2)), jnp.transpose(table_gate, (1, 0, 2)))

def expert_hidden(slot_rows, w_up):
    pre_act = jnp.einsum('imd,hd->imh', slot_rows.astype(jnp.float32), w_up.astype(jnp.float32)) * (1.0 / math.sqrt(D))
    return jax.nn.gelu(pre_act, approximate=True).astype(jnp.bfloat16)

def with_sentinel(values):
    images = values.shape[0]
    return jnp.concatenate([values, jnp.zeros((images, 1, values.shape[2]), values.dtype)], axis=1)

def advance(latent, noise_now, table_token, table_gate, up_all, down_all, section):
    images = latent.shape[0]
    padded = with_sentinel(latent)
    image_index = jnp.arange(images, dtype=jnp.int32)[:, None]

    def one_expert(total, inputs):
        w_up, w_down, token_table, gate_table = inputs
        slot_rows = padded[image_index, token_table]
        hidden = expert_hidden(slot_rows, w_up)
        output = jnp.einsum('imh,hd->imd', hidden.astype(jnp.float32), w_down.astype(jnp.float32)) * (1.0 / math.sqrt(HID))
        output = output.astype(jnp.bfloat16)
        total = total.at[image_index, token_table].add(gate_table[..., None] * output.astype(jnp.float32))
        return (total, None)
    start = jnp.zeros((images, IMG_TOK + 1, D), jnp.float32)
    velocity, unused = lax.scan(one_expert, start, (up_all, down_all, table_token, table_gate))
    keep_gain, drift_gain, noise_gain = coefficients(section)
    moved = keep_gain * latent.astype(jnp.float32) + drift_gain * velocity[:, :IMG_TOK] + noise_gain * noise_now.astype(jnp.float32)
    return moved.astype(jnp.bfloat16)

def reference(latents, noise, expert_ids, gate_values, advantages, expert_pair):
    up_all = expert_pair[:, 0]
    down_all = expert_pair[:, 1]
    tables = [slot_tables(expert_ids[section], gate_values[section]) for section in range(STEPS)]
    history = [latents]
    current = latents
    for section in range(STEPS):
        current = advance(current, noise[section], tables[section][0], tables[section][1], up_all, down_all, section)
        history.append(current)
    images = latents.shape[0]
    image_index = jnp.arange(images, dtype=jnp.int32)[:, None]
    padded_latent = [with_sentinel(history[section]) for section in range(STEPS)]
    padded_noise = [with_sentinel(noise[section]) for section in range(STEPS)]
    scales = []
    for section in range(STEPS):
        keep_gain, drift_gain, noise_gain = coefficients(section)
        scales.append(advantages * (drift_gain / noise_gain))
    token_tables = jnp.stack([tables[section][0] for section in range(STEPS)], axis=1)
    gate_tables = jnp.stack([tables[section][1] for section in range(STEPS)], axis=1)
    rate = 10.0 / math.sqrt(IMG_TOK * TOP * images / EXPERTS)

    def one_expert(carry, inputs):
        w_up, w_down, token_table, gate_table = inputs
        partial_value = jnp.zeros((images, HID, D), jnp.float32)
        for section in range(STEPS):
            slot_rows = padded_latent[section][image_index, token_table[section]]
            hidden = expert_hidden(slot_rows, w_up)
            slot_scale = gate_table[section] * scales[section][:, None]
            slot_noise = padded_noise[section][image_index, token_table[section]]
            cotangent = (slot_scale[..., None] * slot_noise.astype(jnp.float32)).astype(jnp.bfloat16)
            partial_value = partial_value + jnp.einsum('imh,imd->ihd', hidden.astype(jnp.float32), cotangent.astype(jnp.float32))
        grouped = lax.optimization_barrier(jnp.sum(partial_value.reshape(images // IMG_DEV, IMG_DEV, HID, D), axis=1))
        grouped = grouped * (1.0 / math.sqrt(HID))
        rounded = lax.optimization_barrier(grouped.astype(jnp.bfloat16)).astype(jnp.float32)
        updated = (w_down.astype(jnp.float32) + rate * lax.optimization_barrier(jnp.sum(rounded, axis=0))).astype(jnp.bfloat16)
        return (carry, updated)
    unused, new_down = lax.scan(one_expert, jnp.zeros((), jnp.float32), (up_all, down_all, token_tables, gate_tables))
    return (current, new_down)
```

```python
import functools
import math

import jax
import jax.numpy as jnp
from jax import lax
from jax.experimental import pallas as pl
from jax.experimental.pallas import tpu as pltpu
from jax.sharding import PartitionSpec as P

CAP = 7
SIDE = 8
MESH = pl.DeviceIdType.MESH
F32 = jnp.float32
BF16 = jnp.bfloat16


def coefficients(section):
    moment = 0.95 - 0.4 * section
    noise_level = 0.3 * math.sqrt(moment / (1.0 - moment))
    factor = noise_level * noise_level / (2.0 * moment)
    keep_gain = 1.0 - 0.4 * factor
    drift_gain = -0.4 * (1.0 + factor * (1.0 - moment))
    noise_gain = noise_level * math.sqrt(0.4)
    return (keep_gain, drift_gain, noise_gain)


def mm(a, b):
    return jnp.dot(a, b, preferred_element_type=F32)


def iota(shape, dim):
    return lax.broadcasted_iota(jnp.int32, shape, dim)


def kernel(
    sizes,
    ids_ref,
    gate_ref,
    adv_ref,
    lat_ref,
    noise_ref,
    shard_ref,
    fin_ref,
    nd_ref,
    meta_s,
    meta_r,
    gath,
    sel,
    selg,
    selgt,
    scale,
    send_a,
    send_b,
    recv_l,
    recv_n,
    recv_o,
    wbuf,
    perm,
    hid,
    hidp,
    term,
    gx,
    gsend,
    grecv,
    red_r,
    meta_sem,
    gath_sem,
    l_sem,
    n_sem,
    o_sem,
    red_sem,
    wx_sem,
    wc_sem,
    gc_sem,
    gr_sem,
    dx_sem,
    dc_sem,
):
    images, n_role, n_dp, rate = sizes
    toks = lat_ref.shape[0]
    per_image = toks // images
    width = lat_ref.shape[1]
    half = width // 2
    hidden_units = wbuf.shape[1]
    rows = shard_ref.shape[1]
    slots = images * CAP
    blk = SIDE * slots
    total = SIDE * blk
    keep_gain, drift_gain, noise_gain = coefficients(0)

    role = lax.axis_index("role")
    ep = lax.axis_index("ep")
    dp = lax.axis_index("dp")
    z, y = lax.div(ep, SIDE), lax.rem(ep, SIDE)
    other = 1 - dp
    d1 = 1 - 2 * dp
    mine = role * n_dp + dp

    def pos_g(ax):
        return z * (1 - ax) + y * ax

    def pos_x(ax):
        return y * (1 - ax) + z * ax

    def dev_g(ax, i):
        return {"ep": (i * SIDE + y) * (1 - ax) + (z * SIDE + i) * ax}

    def dev_x(ax, i):
        return {"ep": (z * SIDE + i) * (1 - ax) + (i * SIDE + y) * ax}

    def ring(i):
        return lax.rem(i + 2 * SIDE, SIDE)

    def role_at(i):
        return lax.rem(role + n_role + i, n_role)

    def copy(src, dst, sems, at, dev):
        return pltpu.make_async_remote_copy(
            src_ref=src,
            dst_ref=dst,
            send_sem=sems.at[(0,) + at],
            recv_sem=sems.at[(1,) + at],
            device_id=dev,
            device_id_type=MESH,
        )

    def each(low, high, body):
        def step(i, carry):
            body(i)
            return carry

        lax.fori_loop(low, high, step, 0)

    def wrows(q):
        return pl.ds(pl.multiple_of(q * rows, rows), rows)

    def brows(i):
        return pl.ds(pl.multiple_of(i * blk, blk), blk)

    def trows(i):
        return pl.ds(pl.multiple_of(i * toks, toks), toks)

    barrier = pltpu.get_barrier_semaphore()

    def greet(j):
        for ax in (0, 1):
            pl.semaphore_signal(
                barrier, inc=1, device_id=dev_x(ax, ring(pos_x(ax) + j)), device_id_type=MESH
            )

    each(1, SIDE, greet)
    for i in range(1, n_role):
        pl.semaphore_signal(barrier, inc=1, device_id={"role": role_at(i)}, device_id_type=MESH)
    pl.semaphore_signal(barrier, inc=1, device_id={"dp": other}, device_id_type=MESH)

    lane = iota((toks, toks), 1)
    row = iota((toks, toks), 0)
    same = jnp.where(lane >= per_image, 1, 0) == jnp.where(row >= per_image, 1, 0)
    before = jnp.where(same & (row < lane), 1.0, 0.0).astype(BF16)
    first_slot = jnp.where(lane >= per_image, float(CAP), 0.0)
    ids = ids_ref[...]
    gates = gate_ref[...]
    for ax in (0, 1):
        named = ids if ax == 0 else (ids & (SIDE - 1)) * SIDE + (ids >> 3)
        hit = jnp.zeros((toks, toks), F32)
        gate = jnp.zeros((toks, toks), F32)
        for k in range(ids.shape[1]):
            at = named[:, k : k + 1] == lane
            hit = jnp.where(at, 1.0, hit)
            gate = jnp.where(at, gates[:, k : k + 1], gate)
        hit_t = hit.T
        gate_t = gate.T
        rank = mm(hit_t.astype(BF16), before) + first_slot
        place = jnp.where(hit_t > 0.5, rank, -1000.0)
        for i in range(SIDE):
            meta_s[ax, i, 0:SIDE, :] = place[i * SIDE : (i + 1) * SIDE]
            meta_s[ax, i, SIDE : 2 * SIDE, :] = gate_t[i * SIDE : (i + 1) * SIDE]
        cols = slice(ax * half, (ax + 1) * half)
        gath[0, ax, pos_g(ax)] = lat_ref[:, cols]
        gath[1, ax, pos_g(ax)] = noise_ref[:, cols]
        meta_r[ax, pos_g(ax)] = meta_s[ax, pos_g(ax)]
    wbuf[:, wrows(mine), :] = shard_ref[...]

    pl.semaphore_wait(barrier, 2 * (SIDE - 1) + n_role)

    def gath_hop(kind, ax, way, hop):
        step = d1 * (1 - 2 * way)
        slot = ring(pos_g(ax) - step * (hop - 1))
        block = gath.at[kind, ax, slot]
        return copy(block, block, gath_sem, (kind, ax, way, hop - 1), dev_g(ax, ring(pos_g(ax) + step)))

    def gath_wait(kind, ax, way, hop):
        step = d1 * (1 - 2 * way)
        block = gath.at[kind, ax, ring(pos_g(ax) - step * hop)]
        copy(block, block, gath_sem, (kind, ax, way, hop - 1), dev_g(ax, ring(pos_g(ax) + step))).wait_recv()

    def meta_copy(ax, j):
        return copy(
            meta_s.at[ax, ring(pos_g(ax) + j)],
            meta_r.at[ax, pos_g(ax)],
            meta_sem,
            (ax, j - 1),
            dev_g(ax, ring(pos_g(ax) + j)),
        )

    def meta_start(j):
        for ax in (0, 1):
            meta_copy(ax, j).start()

    each(1, SIDE, meta_start)
    for kind in (0, 1):
        for ax in (0, 1):
            for way in (0, 1):
                gath_hop(kind, ax, way, 1).start()

    def w_role(i):
        return copy(shard_ref, wbuf.at[:, wrows(mine), :], wx_sem, (i - 1,), {"role": role_at(i)})

    def w_core(i):
        q = role_at(-i) * n_dp + dp
        block = wbuf.at[:, wrows(q), :]
        return copy(block, block, wc_sem, (i,), {"dp": other})

    for i in range(1, n_role):
        w_role(i).start()
    w_core(0).start()

    def forward(hop):
        for kind in (0, 1):
            for ax in (0, 1):
                for way in (0, 1):
                    if hop <= 4 - way:
                        gath_wait(kind, ax, way, hop)
                        if hop + 1 <= 4 - way:
                            gath_hop(kind, ax, way, hop + 1).start()

    def meta_wait(j):
        for ax in (0, 1):
            slot = meta_r.at[ax, ring(pos_g(ax) - j)]
            copy(slot, slot, meta_sem, (ax, j - 1), dev_g(ax, ring(pos_g(ax) + j))).wait_recv()

    each(1, SIDE, meta_wait)
    gain = drift_gain / noise_gain
    lane1 = iota((1, toks), 1)
    factor = jnp.where(lane1 >= per_image, adv_ref[1] * gain, adv_ref[0] * gain)
    slot_row = iota((blk, toks), 0).astype(F32)

    def build(ax):
        def one(e):
            scaled = jnp.zeros((blk, 1), F32)
            for s in range(SIDE):
                place = meta_r[ax, s, pl.ds(e, 1), :]
                gate = meta_r[ax, s, pl.ds(SIDE + e, 1), :]
                at = (slot_row - float(slots * s)) == place
                cols = slice(s * toks, (s + 1) * toks)
                sel[ax, e, :, cols] = jnp.where(at, 1.0, 0.0).astype(BF16)
                selg[brows(e), cols] = jnp.where(at, gate, 0.0).astype(BF16)
                scaled = scaled + jnp.sum(jnp.where(at, gate * factor, 0.0), axis=1, keepdims=True)
            scale[ax, e] = jnp.broadcast_to(scaled, (blk, toks))

        each(0, SIDE, one)

        def turn(s):
            cols = pl.ds(pl.multiple_of(s * toks, toks), toks)
            for b in range(total // toks):
                part = selg[b * toks : (b + 1) * toks, cols].astype(F32)
                selgt[ax, s, :, b * toks : (b + 1) * toks] = part.T.astype(BF16)

        each(0, SIDE, turn)

    build(0)
    forward(1)
    build(1)
    forward(2)
    r_iota = iota((total, 1), 0)
    outer = lax.div(r_iota, blk)
    inner = lax.div(r_iota - outer * blk, slots)
    target = inner * blk + outer * slots + (r_iota - outer * blk - inner * slots)
    perm[...] = jnp.where(iota((total, total), 1) == target, 1.0, 0.0).astype(BF16)
    forward(3)
    for i in range(1, n_role):
        q = role_at(-i) * n_dp + dp
        block = wbuf.at[:, wrows(q), :]
        copy(block, block, wx_sem, (i - 1,), {"role": role_at(i)}).wait_recv()
        w_core(i).start()
    forward(4)

    def x_copy(buf, dst, sems, ax, j):
        to = ring(pos_x(ax) + j)
        return copy(buf.at[ax, brows(to), :], dst.at[ax, brows(pos_x(ax)), :], sems, (ax, j - 1), dev_x(ax, to))

    def x_wait(dst, sems):
        def one(j):
            for ax in (0, 1):
                block = dst.at[ax, brows(ring(pos_x(ax) - j)), :]
                copy(block, block, sems, (ax, j - 1), dev_x(ax, ring(pos_x(ax) + j))).wait_recv()

        each(1, SIDE, one)

    def x_sent(buf, dst, sems):
        def one(j):
            for ax in (0, 1):
                x_copy(buf, dst, sems, ax, j).wait_send()

        each(1, SIDE, one)

    def picked(kind, ax, e):
        rows_ = gath[kind, ax].reshape(SIDE * toks, half)
        return mm(sel[ax, e], rows_)

    def pack_l(j):
        def one(ax):
            to = ring(pos_x(ax) + j)
            send_a[ax, brows(to), :] = picked(0, ax, to).astype(BF16)
            x_copy(send_a, recv_l, l_sem, ax, j).start()

        each(0, 2, one)

    each(1, SIDE, pack_l)

    def own_l(ax):
        here = pos_x(ax)
        recv_l[ax, brows(here), :] = picked(0, ax, here).astype(BF16)

    each(0, 2, own_l)

    def pack_n(j):
        def one(ax):
            to = ring(pos_x(ax) + j)
            col = scale[ax, to][:, 0:1]
            send_b[ax, brows(to), :] = (col * picked(1, ax, to)).astype(BF16)

        each(0, 2, one)

    each(0, SIDE, pack_n)
    for ax in (0, 1):
        recv_n[ax, brows(pos_x(ax)), :] = send_b[ax, brows(pos_x(ax)), :]
    x_wait(recv_l, l_sem)

    def start_n(j):
        for ax in (0, 1):
            x_copy(send_b, recv_n, n_sem, ax, j).start()

    each(1, SIDE, start_n)

    for i in range(n_role):
        q = role_at(-i) * n_dp + other
        block = wbuf.at[:, wrows(q), :]
        copy(block, block, wc_sem, (i,), {"dp": other}).wait_recv()
    x_sent(send_a, recv_l, l_sem)
    chunk = 256

    def cols_at(n):
        return pl.ds(pl.multiple_of(n * chunk, chunk), chunk)

    def align(n):
        send_a[1, :, cols_at(n)] = mm(perm[...], recv_l[1, :, cols_at(n)]).astype(BF16)

    each(0, half // chunk, align)

    def up(n):
        def nt(a, b):
            return lax.dot_general(a, b, (((1,), (1,)), ((), ())), preferred_element_type=F32)

        hrows = pl.ds(pl.multiple_of(n * chunk, chunk), chunk)
        pre = nt(recv_l[0], wbuf[0, hrows, 0:half]) + nt(send_a[1], wbuf[0, hrows, half:width])
        hidden = jax.nn.gelu(pre * (1.0 / math.sqrt(width)), approximate=True).astype(BF16)
        hid[:, cols_at(n)] = hidden
        hidp[:, cols_at(n)] = mm(perm[...], hidden).astype(BF16)

    each(0, hidden_units // chunk, up)
    down_gain = 1.0 / math.sqrt(hidden_units)

    for ax in (0, 1):
        source = hid if ax == 0 else hidp

        def down(n, ax=ax, source=source):
            cols = pl.ds(pl.multiple_of(ax * half + n * chunk, chunk), chunk)
            send_a[ax, :, cols_at(n)] = (mm(source[...], wbuf[1, :, cols]) * down_gain).astype(BF16)

        each(0, half // chunk, down)

        def start_o(j, ax=ax):
            x_copy(send_a, recv_o, o_sem, ax, j).start()

        each(1, SIDE, start_o)
        recv_o[ax, brows(pos_x(ax)), :] = send_a[ax, brows(pos_x(ax)), :]

    x_wait(recv_n, n_sem)
    for ax in (0, 1):
        source = hid if ax == 0 else hidp

        def outer_product(m, ax=ax, source=source):
            part = lax.dot_general(
                source[:, cols_at(m)], recv_n[ax], (((0,), (0,)), ((), ())), preferred_element_type=F32
            )
            mrows = pl.ds(pl.multiple_of(m * chunk, chunk), chunk)
            term[mrows, ax * half : (ax + 1) * half] = (part * down_gain).astype(BF16)

        each(0, hidden_units // chunk, outer_product)

    def g_core(i):
        return copy(term.at[wrows(i * n_dp + other), :], gx.at[i], gc_sem, (i,), {"dp": other})

    for i in range(n_role):
        g_core(i).start()
    x_sent(send_b, recv_n, n_sem)

    def weighed(ax, to):
        return mm(selgt[ax, to], recv_o[ax])

    def red_slot(way, k):
        return way * 4 + k - 1

    def red_copy(ax, way, k):
        step = d1 * (1 - 2 * way)
        slot = red_slot(way, k)
        return copy(
            send_b.at[ax, trows(slot), :],
            red_r.at[ax, trows(slot), :],
            red_sem,
            (ax, slot),
            dev_g(ax, ring(pos_g(ax) + step)),
        )

    def red_arrived(ax, way, k):
        slot = red_slot(way, k)
        block = red_r.at[ax, trows(slot), :]
        copy(block, block, red_sem, (ax, slot), dev_g(ax, ring(pos_g(ax) + d1 * (1 - 2 * way)))).wait_recv()
        return red_r[ax, trows(slot), :].astype(F32)

    def reduce_step(k):
        def one(ax):
            for way in (0, 1):
                hops = 4 - way
                if k > hops:
                    continue
                step = d1 * (1 - 2 * way)
                value = weighed(ax, ring(pos_g(ax) + step * (hops + 1 - k)))
                if k > 1:
                    value = value + red_arrived(ax, way, k - 1)
                send_b[ax, trows(red_slot(way, k)), :] = value.astype(BF16)
                red_copy(ax, way, k).start()

        each(0, 2, one)

    x_wait(recv_o, o_sem)
    reduce_step(1)

    def g_role(i):
        return copy(gsend.at[i - 1], grecv.at[i - 1], gr_sem, (i - 1,), {"role": role_at(i)})

    for i in range(n_role):
        copy(gx.at[i], gx.at[i], gc_sem, (i,), {"dp": other}).wait_recv()
    for i in range(1, n_role):
        to = role_at(i)
        gsend[i - 1] = (term[wrows(to * n_dp + dp), :].astype(F32) + gx[to].astype(F32)).astype(BF16)
        g_role(i).start()

    reduce_step(2)
    reduce_step(3)

    for i in range(1, n_role):
        copy(grecv.at[i - 1], grecv.at[i - 1], gr_sem, (i - 1,), {"role": role_at(i)}).wait_recv()
    grad = term[wrows(mine), :].astype(F32) + gx[role].astype(F32)
    for i in range(1, n_role):
        grad = grad + grecv[i - 1].astype(F32)
    nd_ref[wrows(mine), :] = (wbuf[1, wrows(mine), :].astype(F32) + rate * grad).astype(BF16)

    def d_role(i):
        block = nd_ref.at[wrows(mine), :]
        return copy(block, block, dx_sem, (i - 1,), {"role": role_at(i)})

    def d_core(i):
        block = nd_ref.at[wrows(role_at(-i) * n_dp + dp), :]
        return copy(block, block, dc_sem, (i,), {"dp": other})

    for i in range(1, n_role):
        d_role(i).start()
    d_core(0).start()

    reduce_step(4)

    for i in range(1, n_role):
        block = nd_ref.at[wrows(role_at(-i) * n_dp + dp), :]
        copy(block, block, dx_sem, (i - 1,), {"role": role_at(i)}).wait_recv()
        d_core(i).start()

    for ax in (0, 1):
        cols = slice(ax * half, (ax + 1) * half)
        velocity = weighed(ax, pos_g(ax)) + red_arrived(ax, 1, 3) + red_arrived(ax, 0, 4)
        moved = (
            keep_gain * lat_ref[:, cols].astype(F32)
            + drift_gain * velocity
            + noise_gain * noise_ref[:, cols].astype(F32)
        )
        fin_ref[:, cols] = moved.astype(BF16)

    for i in range(n_role):
        block = nd_ref.at[wrows(role_at(-i) * n_dp + other), :]
        copy(block, block, dc_sem, (i,), {"dp": other}).wait_recv()

    def meta_sent(j):
        for ax in (0, 1):
            meta_copy(ax, j).wait_send()

    each(1, SIDE, meta_sent)
    for kind in (0, 1):
        for ax in (0, 1):
            for way in (0, 1):
                for hop in range(1, 5 - way):
                    gath_hop(kind, ax, way, hop).wait_send()
    x_sent(send_a, recv_o, o_sem)
    for ax in (0, 1):
        for way in (0, 1):
            for k in range(1, 5 - way):
                red_copy(ax, way, k).wait_send()
    for i in range(1, n_role):
        w_role(i).wait_send()
        g_role(i).wait_send()
        d_role(i).wait_send()
    for i in range(n_role):
        w_core(i).wait_send()
        g_core(i).wait_send()
        d_core(i).wait_send()


def per_device(latents, noise, expert_ids, gate_values, advantages, expert_pair):
    n_role, n_dp, n_ep = lax.axis_size("role"), lax.axis_size("dp"), lax.axis_size("ep")
    images, tok_count, width = latents.shape
    top = expert_ids.shape[3]
    toks = images * tok_count
    rows = expert_pair.shape[2]
    hidden_units = rows * n_role * n_dp
    experts = expert_pair.shape[0] * n_ep
    half = width // 2
    slots = images * CAP
    blk = SIDE * slots
    total = SIDE * blk
    rate = 10.0 / math.sqrt(tok_count * n_ep * top * images * n_role * n_dp / experts)
    vmem = pl.BlockSpec(memory_space=pltpu.VMEM)
    dma = pltpu.SemaphoreType.DMA
    fin, new_down = pl.pallas_call(
        functools.partial(kernel, (images, n_role, n_dp, rate)),
        out_shape=(
            jax.ShapeDtypeStruct((toks, width), BF16),
            jax.ShapeDtypeStruct((hidden_units, width), BF16),
        ),
        in_specs=[vmem, vmem, pl.BlockSpec(memory_space=pltpu.SMEM), vmem, vmem, vmem],
        out_specs=(vmem, vmem),
        scratch_shapes=[
            pltpu.VMEM((2, SIDE, 2 * SIDE, toks), F32),
            pltpu.VMEM((2, SIDE, 2 * SIDE, toks), F32),
            pltpu.VMEM((2, 2, SIDE, toks, half), BF16),
            pltpu.VMEM((2, SIDE, blk, SIDE * toks), BF16),
            pltpu.VMEM((total, SIDE * toks), BF16),
            pltpu.VMEM((2, SIDE, toks, total), BF16),
            pltpu.VMEM((2, SIDE, blk, toks), F32),
            pltpu.VMEM((2, total, half), BF16),
            pltpu.VMEM((2, total, half), BF16),
            pltpu.VMEM((2, total, half), BF16),
            pltpu.VMEM((2, total, half), BF16),
            pltpu.VMEM((2, total, half), BF16),
            pltpu.VMEM((2, hidden_units, width), BF16),
            pltpu.VMEM((total, total), BF16),
            pltpu.VMEM((total, hidden_units), BF16),
            pltpu.VMEM((total, hidden_units), BF16),
            pltpu.VMEM((hidden_units, width), BF16),
            pltpu.VMEM((n_role, rows, width), BF16),
            pltpu.VMEM((n_role - 1, rows, width), BF16),
            pltpu.VMEM((n_role - 1, rows, width), BF16),
            pltpu.VMEM((2, 7 * toks, half), BF16),
            dma((2, 2, SIDE - 1)),
            dma((2, 2, 2, 2, 4)),
            dma((2, 2, SIDE - 1)),
            dma((2, 2, SIDE - 1)),
            dma((2, 2, SIDE - 1)),
            dma((2, 2, 7)),
            dma((2, n_role - 1)),
            dma((2, n_role)),
            dma((2, n_role)),
            dma((2, n_role - 1)),
            dma((2, n_role - 1)),
            dma((2, n_role)),
        ],
        compiler_params=pltpu.CompilerParams(
            collective_id=0, has_side_effects=True, vmem_limit_bytes=60 * 1024 * 1024
        ),
    )(
        expert_ids.reshape(toks, top),
        gate_values.reshape(toks, top),
        advantages,
        latents.reshape(toks, width),
        noise.reshape(toks, width),
        expert_pair.reshape(2, rows, width),
    )
    return (fin.reshape(images, tok_count, width), new_down.reshape(1, hidden_units, width))


def solution(mesh):
    in_specs = (
        P(("role", "dp"), "ep", None),
        P(None, ("role", "dp"), "ep", None),
        P(None, ("role", "dp"), "ep", None),
        P(None, ("role", "dp"), "ep", None),
        P(("role", "dp")),
        P("ep", None, ("role", "dp"), None),
    )
    out_specs = (P(("role", "dp"), "ep", None), P("ep", None, None))
    return jax.shard_map(
        per_device, mesh=mesh, in_specs=in_specs, out_specs=out_specs, check_vma=False
    )
```

```python
import functools
import math

import jax
import jax.numpy as jnp
from jax import lax
from jax.experimental import pallas as pl
from jax.experimental.pallas import tpu as pltpu
from jax.sharding import PartitionSpec as P

CAP = 7
SIDE = 8
MESH = pl.DeviceIdType.MESH
F32 = jnp.float32
BF16 = jnp.bfloat16


def coefficients(section):
    moment = 0.95 - 0.4 * section
    noise_level = 0.3 * math.sqrt(moment / (1.0 - moment))
    factor = noise_level * noise_level / (2.0 * moment)
    keep_gain = 1.0 - 0.4 * factor
    drift_gain = -0.4 * (1.0 + factor * (1.0 - moment))
    noise_gain = noise_level * math.sqrt(0.4)
    return (keep_gain, drift_gain, noise_gain)


def mm(a, b):
    return jnp.dot(a, b, preferred_element_type=F32)


def iota(shape, dim):
    return lax.broadcasted_iota(jnp.int32, shape, dim)


def kernel(
    sizes,
    ids_ref,
    gate_ref,
    adv_ref,
    lat_ref,
    noise_ref,
    shard_ref,
    fin_ref,
    nd_ref,
    meta_s,
    meta_r,
    gath,
    sel,
    selg,
    selgt,
    scale,
    send_a,
    send_b,
    recv_l,
    recv_n,
    recv_o,
    wbuf,
    perm,
    hid,
    hidp,
    term,
    gx,
    gsend,
    grecv,
    red_r,
    vel,
    meta_sem,
    gath_sem,
    l_sem,
    n_sem,
    o_sem,
    red_sem,
    wx_sem,
    wc_sem,
    gc_sem,
    gr_sem,
    dx_sem,
    dc_sem,
):
    images, n_role, n_dp, rate = sizes
    toks = lat_ref.shape[0]
    per_image = toks // images
    width = lat_ref.shape[1]
    half = width // 2
    hidden_units = wbuf.shape[1]
    rows = shard_ref.shape[1]
    slots = images * CAP
    blk = SIDE * slots
    total = SIDE * blk
    keep_gain, drift_gain, noise_gain = coefficients(0)

    role = lax.axis_index("role")
    ep = lax.axis_index("ep")
    dp = lax.axis_index("dp")
    z, y = lax.div(ep, SIDE), lax.rem(ep, SIDE)
    other = 1 - dp
    d1 = 1 - 2 * dp
    mine = role * n_dp + dp

    def pos_g(ax):
        return z * (1 - ax) + y * ax

    def pos_x(ax):
        return y * (1 - ax) + z * ax

    def dev_g(ax, i):
        return {"ep": (i * SIDE + y) * (1 - ax) + (z * SIDE + i) * ax}

    def dev_x(ax, i):
        return {"ep": (z * SIDE + i) * (1 - ax) + (i * SIDE + y) * ax}

    def ring(i):
        return lax.rem(i + 2 * SIDE, SIDE)

    def role_at(i):
        return lax.rem(role + n_role + i, n_role)

    def copy(src, dst, sems, at, dev):
        return pltpu.make_async_remote_copy(
            src_ref=src,
            dst_ref=dst,
            send_sem=sems.at[(0,) + at],
            recv_sem=sems.at[(1,) + at],
            device_id=dev,
            device_id_type=MESH,
        )

    def each(low, high, body):
        def step(i, carry):
            body(i)
            return carry

        lax.fori_loop(low, high, step, 0)

    def wrows(q):
        return pl.ds(pl.multiple_of(q * rows, rows), rows)

    def brows(i):
        return pl.ds(pl.multiple_of(i * blk, blk), blk)

    def trows(i):
        return pl.ds(pl.multiple_of(i * toks, toks), toks)

    barrier = pltpu.get_barrier_semaphore()

    def greet(j):
        for ax in (0, 1):
            pl.semaphore_signal(
                barrier, inc=1, device_id=dev_x(ax, ring(pos_x(ax) + j)), device_id_type=MESH
            )

    each(1, SIDE, greet)
    for i in range(1, n_role):
        pl.semaphore_signal(barrier, inc=1, device_id={"role": role_at(i)}, device_id_type=MESH)
    pl.semaphore_signal(barrier, inc=1, device_id={"dp": other}, device_id_type=MESH)

    for ax in (0, 1):
        cols = slice(ax * half, (ax + 1) * half)
        gath[0, ax, pos_g(ax)] = lat_ref[:, cols]
        gath[1, ax, pos_g(ax)] = noise_ref[:, cols]

    pl.semaphore_wait(barrier, 2 * (SIDE - 1) + n_role)

    def gath_hop(kind, ax, way, hop):
        step = d1 * (1 - 2 * way)
        slot = ring(pos_g(ax) - step * (hop - 1))
        block = gath.at[kind, ax, slot]
        return copy(block, block, gath_sem, (kind, ax, way, hop - 1), dev_g(ax, ring(pos_g(ax) + step)))

    def gath_wait(kind, ax, way, hop):
        step = d1 * (1 - 2 * way)
        block = gath.at[kind, ax, ring(pos_g(ax) - step * hop)]
        copy(block, block, gath_sem, (kind, ax, way, hop - 1), dev_g(ax, ring(pos_g(ax) + step))).wait_recv()

    def meta_copy(ax, j):
        return copy(
            meta_s.at[ax, ring(pos_g(ax) + j)],
            meta_r.at[ax, pos_g(ax)],
            meta_sem,
            (ax, j - 1),
            dev_g(ax, ring(pos_g(ax) + j)),
        )

    def meta_start(j):
        for ax in (0, 1):
            meta_copy(ax, j).start()

    for kind in (0, 1):
        for ax in (0, 1):
            for way in (0, 1):
                gath_hop(kind, ax, way, 1).start()

    def w_role(i):
        return copy(shard_ref, wbuf.at[:, wrows(mine), :], wx_sem, (i - 1,), {"role": role_at(i)})

    def w_core(i):
        q = role_at(-i) * n_dp + dp
        block = wbuf.at[:, wrows(q), :]
        return copy(block, block, wc_sem, (i,), {"dp": other})

    for i in range(1, n_role):
        w_role(i).start()

    row = iota((toks, toks), 0)
    lane = iota((toks, toks), 1)
    same = jnp.where(lane >= per_image, 1, 0) == jnp.where(row >= per_image, 1, 0)
    before = jnp.where(same & (row < lane), 1.0, 0.0).astype(BF16)
    experts = SIDE * SIDE
    expert_row = iota((experts, toks), 0)
    first_slot = jnp.where(iota((experts, toks), 1) >= per_image, float(CAP), 0.0)
    for ax in (0, 1):
        hit = jnp.zeros((experts, toks), F32)
        gate = jnp.zeros((experts, toks), F32)
        for k in range(ids_ref.shape[0]):
            named = jnp.concatenate([ids_ref[k, i : i + 1, :] for i in range(images)], axis=1)
            weight = jnp.concatenate([gate_ref[k, i : i + 1, :] for i in range(images)], axis=1)
            if ax == 1:
                named = (named & (SIDE - 1)) * SIDE + (named >> 3)
            at = named == expert_row
            hit = jnp.where(at, 1.0, hit)
            gate = jnp.where(at, weight, gate)
        place = jnp.where(hit > 0.5, mm(hit.astype(BF16), before) + first_slot, -1000.0)
        for i in range(SIDE):
            meta_s[ax, i, 0:SIDE, :] = place[i * SIDE : (i + 1) * SIDE]
            meta_s[ax, i, SIDE : 2 * SIDE, :] = gate[i * SIDE : (i + 1) * SIDE]
        meta_r[ax, pos_g(ax)] = meta_s[ax, pos_g(ax)]
    each(1, SIDE, meta_start)
    wbuf[:, wrows(mine), :] = shard_ref[...]
    w_core(0).start()

    def forward(kind, hop):
        for ax in (0, 1):
            for way in (0, 1):
                if hop <= 4 - way:
                    gath_wait(kind, ax, way, hop)
                    if hop + 1 <= 4 - way:
                        gath_hop(kind, ax, way, hop + 1).start()

    def meta_wait(j):
        for ax in (0, 1):
            slot = meta_r.at[ax, ring(pos_g(ax) - j)]
            copy(slot, slot, meta_sem, (ax, j - 1), dev_g(ax, ring(pos_g(ax) + j))).wait_recv()

    forward(0, 1)
    each(1, SIDE, meta_wait)
    gain = drift_gain / noise_gain
    lane1 = iota((1, toks), 1)
    factor = jnp.where(lane1 >= per_image, adv_ref[1] * gain, adv_ref[0] * gain)
    slot_row = iota((blk, toks), 0).astype(F32)

    def build(ax):
        def one(e):
            scaled = jnp.zeros((blk, 1), F32)
            for s in range(SIDE):
                place = meta_r[ax, s, pl.ds(e, 1), :]
                gate = meta_r[ax, s, pl.ds(SIDE + e, 1), :]
                at = (slot_row - float(slots * s)) == place
                cols = slice(s * toks, (s + 1) * toks)
                sel[ax, e, :, cols] = jnp.where(at, 1.0, 0.0).astype(BF16)
                selg[brows(e), cols] = jnp.where(at, gate, 0.0).astype(BF16)
                scaled = scaled + jnp.sum(jnp.where(at, gate * factor, 0.0), axis=1, keepdims=True)
            scale[ax, e] = jnp.broadcast_to(scaled, (blk, toks))

        each(0, SIDE, one)

        def turn(s):
            cols = pl.ds(pl.multiple_of(s * toks, toks), toks)
            for b in range(total // toks):
                part = selg[b * toks : (b + 1) * toks, cols].astype(F32)
                selgt[ax, s, :, b * toks : (b + 1) * toks] = part.T.astype(BF16)

        each(0, SIDE, turn)

    build(0)
    forward(1, 1)
    forward(0, 2)
    build(1)
    forward(1, 2)
    forward(0, 3)
    r_iota = iota((total, 1), 0)
    outer = lax.div(r_iota, blk)
    inner = lax.div(r_iota - outer * blk, slots)
    target = inner * blk + outer * slots + (r_iota - outer * blk - inner * slots)
    perm[...] = jnp.where(iota((total, total), 1) == target, 1.0, 0.0).astype(BF16)
    forward(1, 3)
    for i in range(1, n_role):
        q = role_at(-i) * n_dp + dp
        block = wbuf.at[:, wrows(q), :]
        copy(block, block, wx_sem, (i - 1,), {"role": role_at(i)}).wait_recv()
        w_core(i).start()
    forward(0, 4)

    everything = (0, half)

    def x_copy(buf, dst, sems, ax, j, pre=(), cols=everything):
        to = ring(pos_x(ax) + j)
        lanes = slice(*cols)
        return copy(
            buf.at[ax, brows(to), lanes], dst.at[ax, brows(pos_x(ax)), lanes], sems, pre + (ax, j - 1), dev_x(ax, to)
        )

    def x_wait(dst, sems, pre=(), cols=everything, low=1, high=SIDE):
        def one(j):
            for ax in (0, 1):
                block = dst.at[ax, brows(ring(pos_x(ax) - j)), slice(*cols)]
                copy(block, block, sems, pre + (ax, j - 1), dev_x(ax, ring(pos_x(ax) + j))).wait_recv()

        each(low, high, one)

    def x_sent(buf, dst, sems, pre=(), cols=everything):
        def one(j):
            for ax in (0, 1):
                x_copy(buf, dst, sems, ax, j, pre, cols).wait_send()

        each(1, SIDE, one)

    def far_first(body):
        def one(i):
            body(SIDE // 2 + (2 * lax.rem(i, 2) - 1) * lax.div(i, 2))

        each(1, SIDE, one)

    def picked(kind, ax, e):
        rows_ = gath[kind, ax].reshape(SIDE * toks, half)
        return mm(sel[ax, e], rows_)

    def pack_l(j):
        def one(ax):
            to = ring(pos_x(ax) + j)
            send_a[ax, brows(to), :] = picked(0, ax, to).astype(BF16)
            x_copy(send_a, recv_l, l_sem, ax, j).start()

        each(0, 2, one)

    far_first(pack_l)

    def own_l(ax):
        here = pos_x(ax)
        recv_l[ax, brows(here), :] = picked(0, ax, here).astype(BF16)

    each(0, 2, own_l)

    def pack_n(j):
        def one(ax):
            to = ring(pos_x(ax) + j)
            col = scale[ax, to][:, 0:1]
            send_b[ax, brows(to), :] = (col * picked(1, ax, to)).astype(BF16)

        each(0, 2, one)

    forward(1, 4)
    each(0, SIDE, pack_n)
    for ax in (0, 1):
        recv_n[ax, brows(pos_x(ax)), :] = send_b[ax, brows(pos_x(ax)), :]

    def start_n(j):
        for ax in (0, 1):
            x_copy(send_b, recv_n, n_sem, ax, j).start()

    far_first(start_n)
    x_wait(recv_l, l_sem)

    for i in range(n_role):
        q = role_at(-i) * n_dp + other
        block = wbuf.at[:, wrows(q), :]
        copy(block, block, wc_sem, (i,), {"dp": other}).wait_recv()
    x_sent(send_a, recv_l, l_sem)
    chunk = 256

    def cols_at(n):
        return pl.ds(pl.multiple_of(n * chunk, chunk), chunk)

    def align(n):
        send_a[1, :, cols_at(n)] = mm(perm[...], recv_l[1, :, cols_at(n)]).astype(BF16)

    each(0, half // chunk, align)

    def up(n):
        def nt(a, b):
            return lax.dot_general(a, b, (((1,), (1,)), ((), ())), preferred_element_type=F32)

        hrows = pl.ds(pl.multiple_of(n * chunk, chunk), chunk)
        pre = nt(recv_l[0], wbuf[0, hrows, 0:half]) + nt(send_a[1], wbuf[0, hrows, half:width])
        hidden = jax.nn.gelu(pre * (1.0 / math.sqrt(width)), approximate=True).astype(BF16)
        hid[:, cols_at(n)] = hidden
        hidp[:, cols_at(n)] = mm(perm[...], hidden).astype(BF16)

    each(0, hidden_units // chunk, up)
    down_gain = 1.0 / math.sqrt(hidden_units)

    parts = ((0, chunk), (chunk, half))

    for part, cols in enumerate(parts):
        for ax in (0, 1):
            source = hid if ax == 0 else hidp

            def down(n, ax=ax, source=source):
                lanes = pl.ds(pl.multiple_of(ax * half + n * chunk, chunk), chunk)
                send_a[ax, :, cols_at(n)] = (mm(source[...], wbuf[1, :, lanes]) * down_gain).astype(BF16)

            each(cols[0] // chunk, cols[1] // chunk, down)

            def start_o(j, ax=ax, part=part, cols=cols):
                x_copy(send_a, recv_o, o_sem, ax, j, (part,), cols).start()

            far_first(start_o)
    for ax in (0, 1):
        recv_o[ax, brows(pos_x(ax)), :] = send_a[ax, brows(pos_x(ax)), :]

    x_wait(recv_n, n_sem)
    for ax in (0, 1):
        source = hid if ax == 0 else hidp

        def outer_product(m, ax=ax, source=source):
            part = lax.dot_general(
                source[:, cols_at(m)], recv_n[ax], (((0,), (0,)), ((), ())), preferred_element_type=F32
            )
            mrows = pl.ds(pl.multiple_of(m * chunk, chunk), chunk)
            term[mrows, ax * half : (ax + 1) * half] = (part * down_gain).astype(BF16)

        each(0, hidden_units // chunk, outer_product)

    def g_core(i):
        return copy(term.at[wrows(i * n_dp + other), :], gx.at[i], gc_sem, (i,), {"dp": other})

    for i in range(n_role):
        g_core(i).start()

    def g_role(i):
        return copy(gsend.at[i - 1], grecv.at[i - 1], gr_sem, (i - 1,), {"role": role_at(i)})

    for i in range(n_role):
        copy(gx.at[i], gx.at[i], gc_sem, (i,), {"dp": other}).wait_recv()
    for i in range(1, n_role):
        to = role_at(i)
        gsend[i - 1] = (term[wrows(to * n_dp + dp), :].astype(F32) + gx[to].astype(F32)).astype(BF16)
        g_role(i).start()

    def weighed(part, ax, to):
        return mm(selgt[ax, to], recv_o[ax, :, slice(*parts[part])])

    def red_slot(way, k):
        return way * 4 + k - 1

    def red_copy(part, ax, way, k):
        step = d1 * (1 - 2 * way)
        slot = red_slot(way, k)
        lanes = slice(*parts[part])
        return copy(
            send_b.at[ax, trows(slot), lanes],
            red_r.at[ax, trows(slot), lanes],
            red_sem,
            (part, ax, slot),
            dev_g(ax, ring(pos_g(ax) + step)),
        )

    def red_arrived(part, ax, way, k):
        slot = red_slot(way, k)
        lanes = slice(*parts[part])
        block = red_r.at[ax, trows(slot), lanes]
        to = dev_g(ax, ring(pos_g(ax) + d1 * (1 - 2 * way)))
        copy(block, block, red_sem, (part, ax, slot), to).wait_recv()
        return red_r[ax, trows(slot), lanes].astype(F32)

    def prepare(part, k):
        def one(ax):
            for way in (0, 1):
                hops = 4 - way
                if k > hops and not (k == 5 and way == 0):
                    continue
                step = d1 * (1 - 2 * way)
                vel[ax, way, :, slice(*parts[part])] = weighed(part, ax, ring(pos_g(ax) + step * (hops + 1 - k)))

        each(0, 2, one)

    def push(part, k):
        lanes = slice(*parts[part])

        def one(ax):
            for way in (0, 1):
                if k > 4 - way:
                    continue
                value = vel[ax, way, :, lanes]
                if k > 1:
                    value = value + red_arrived(part, ax, way, k - 1)
                send_b[ax, trows(red_slot(way, k)), lanes] = value.astype(BF16)
                red_copy(part, ax, way, k).start()

        each(0, 2, one)
        prepare(part, k + 1)

    def finish(part):
        low, high = parts[part]
        for ax in (0, 1):
            cols = slice(ax * half + low, ax * half + high)
            velocity = vel[ax, 0, :, low:high] + red_arrived(part, ax, 1, 3) + red_arrived(part, ax, 0, 4)
            moved = (
                keep_gain * lat_ref[:, cols].astype(F32)
                + drift_gain * velocity
                + noise_gain * noise_ref[:, cols].astype(F32)
            )
            fin_ref[:, cols] = moved.astype(BF16)

    x_wait(recv_o, o_sem, (0,), parts[0])
    x_sent(send_b, recv_n, n_sem)
    prepare(0, 1)
    push(0, 1)
    push(0, 2)

    for i in range(1, n_role):
        copy(grecv.at[i - 1], grecv.at[i - 1], gr_sem, (i - 1,), {"role": role_at(i)}).wait_recv()
    grad = term[wrows(mine), :].astype(F32) + gx[role].astype(F32)
    for i in range(1, n_role):
        grad = grad + grecv[i - 1].astype(F32)
    nd_ref[wrows(mine), :] = (wbuf[1, wrows(mine), :].astype(F32) + rate * grad).astype(BF16)

    def d_role(i):
        block = nd_ref.at[wrows(mine), :]
        return copy(block, block, dx_sem, (i - 1,), {"role": role_at(i)})

    def d_core(i):
        block = nd_ref.at[wrows(role_at(-i) * n_dp + dp), :]
        return copy(block, block, dc_sem, (i,), {"dp": other})

    for i in range(1, n_role):
        d_role(i).start()
    d_core(0).start()

    push(0, 3)
    x_wait(recv_o, o_sem, (1,), parts[1])
    prepare(1, 1)
    push(1, 1)
    push(0, 4)
    push(1, 2)

    for i in range(1, n_role):
        block = nd_ref.at[wrows(role_at(-i) * n_dp + dp), :]
        copy(block, block, dx_sem, (i - 1,), {"role": role_at(i)}).wait_recv()
        d_core(i).start()

    push(1, 3)
    push(1, 4)
    finish(0)
    finish(1)

    for i in range(n_role):
        block = nd_ref.at[wrows(role_at(-i) * n_dp + other), :]
        copy(block, block, dc_sem, (i,), {"dp": other}).wait_recv()

    def meta_sent(j):
        for ax in (0, 1):
            meta_copy(ax, j).wait_send()

    each(1, SIDE, meta_sent)
    for kind in (0, 1):
        for ax in (0, 1):
            for way in (0, 1):
                for hop in range(1, 5 - way):
                    gath_hop(kind, ax, way, hop).wait_send()
    for part, cols in enumerate(parts):
        x_sent(send_a, recv_o, o_sem, (part,), cols)
    for part in range(len(parts)):
        for ax in (0, 1):
            for way in (0, 1):
                for k in range(1, 5 - way):
                    red_copy(part, ax, way, k).wait_send()
    for i in range(1, n_role):
        w_role(i).wait_send()
        g_role(i).wait_send()
        d_role(i).wait_send()
    for i in range(n_role):
        w_core(i).wait_send()
        g_core(i).wait_send()
        d_core(i).wait_send()


def per_device(latents, noise, expert_ids, gate_values, advantages, expert_pair):
    n_role, n_dp, n_ep = lax.axis_size("role"), lax.axis_size("dp"), lax.axis_size("ep")
    images, tok_count, width = latents.shape
    top = expert_ids.shape[3]
    toks = images * tok_count
    rows = expert_pair.shape[2]
    hidden_units = rows * n_role * n_dp
    experts = expert_pair.shape[0] * n_ep
    half = width // 2
    slots = images * CAP
    blk = SIDE * slots
    total = SIDE * blk
    rate = 10.0 / math.sqrt(tok_count * n_ep * top * images * n_role * n_dp / experts)
    vmem = pl.BlockSpec(memory_space=pltpu.VMEM)
    dma = pltpu.SemaphoreType.DMA
    fin, new_down = pl.pallas_call(
        functools.partial(kernel, (images, n_role, n_dp, rate)),
        out_shape=(
            pltpu.VMEM((toks, width), BF16),
            pltpu.VMEM((hidden_units, width), BF16),
        ),
        in_specs=[vmem, vmem, pl.BlockSpec(memory_space=pltpu.SMEM), vmem, vmem, vmem],
        out_specs=(vmem, vmem),
        scratch_shapes=[
            pltpu.VMEM((2, SIDE, 2 * SIDE, toks), F32),
            pltpu.VMEM((2, SIDE, 2 * SIDE, toks), F32),
            pltpu.VMEM((2, 2, SIDE, toks, half), BF16),
            pltpu.VMEM((2, SIDE, blk, SIDE * toks), BF16),
            pltpu.VMEM((total, SIDE * toks), BF16),
            pltpu.VMEM((2, SIDE, toks, total), BF16),
            pltpu.VMEM((2, SIDE, blk, toks), F32),
            pltpu.VMEM((2, total, half), BF16),
            pltpu.VMEM((2, total, half), BF16),
            pltpu.VMEM((2, total, half), BF16),
            pltpu.VMEM((2, total, half), BF16),
            pltpu.VMEM((2, total, half), BF16),
            pltpu.VMEM((2, hidden_units, width), BF16),
            pltpu.VMEM((total, total), BF16),
            pltpu.VMEM((total, hidden_units), BF16),
            pltpu.VMEM((total, hidden_units), BF16),
            pltpu.VMEM((hidden_units, width), BF16),
            pltpu.VMEM((n_role, rows, width), BF16),
            pltpu.VMEM((n_role - 1, rows, width), BF16),
            pltpu.VMEM((n_role - 1, rows, width), BF16),
            pltpu.VMEM((2, 7 * toks, half), BF16),
            pltpu.VMEM((2, 2, toks, half), F32),
            dma((2, 2, SIDE - 1)),
            dma((2, 2, 2, 2, 4)),
            dma((2, 2, SIDE - 1)),
            dma((2, 2, SIDE - 1)),
            dma((2, 2, 2, SIDE - 1)),
            dma((2, 2, 2, 7)),
            dma((2, n_role - 1)),
            dma((2, n_role)),
            dma((2, n_role)),
            dma((2, n_role - 1)),
            dma((2, n_role - 1)),
            dma((2, n_role)),
        ],
        compiler_params=pltpu.CompilerParams(
            collective_id=0, has_side_effects=True, vmem_limit_bytes=56 * 1024 * 1024
        ),
    )(
        jnp.transpose(expert_ids[0], (2, 0, 1)),
        jnp.transpose(gate_values[0], (2, 0, 1)),
        advantages,
        latents.reshape(toks, width),
        noise.reshape(toks, width),
        expert_pair.reshape(2, rows, width),
    )
    return (fin.reshape(images, tok_count, width), new_down.reshape(1, hidden_units, width))


def solution(mesh):
    in_specs = (
        P(("role", "dp"), "ep", None),
        P(None, ("role", "dp"), "ep", None),
        P(None, ("role", "dp"), "ep", None),
        P(None, ("role", "dp"), "ep", None),
        P(("role", "dp")),
        P("ep", None, ("role", "dp"), None),
    )
    out_specs = (P(("role", "dp"), "ep", None), P("ep", None, None))
    return jax.shard_map(
        per_device, mesh=mesh, in_specs=in_specs, out_specs=out_specs, check_vma=False
    )
```

```python
import functools
import math

import jax
import jax.numpy as jnp
from jax import lax
from jax.experimental import pallas as pl
from jax.experimental.pallas import tpu as pltpu
from jax.sharding import PartitionSpec as P

CAP = 7
SIDE = 8
MESH = pl.DeviceIdType.MESH
F32 = jnp.float32
BF16 = jnp.bfloat16


def coefficients(section):
    moment = 0.95 - 0.4 * section
    noise_level = 0.3 * math.sqrt(moment / (1.0 - moment))
    factor = noise_level * noise_level / (2.0 * moment)
    keep_gain = 1.0 - 0.4 * factor
    drift_gain = -0.4 * (1.0 + factor * (1.0 - moment))
    noise_gain = noise_level * math.sqrt(0.4)
    return (keep_gain, drift_gain, noise_gain)


def mm(a, b):
    return jnp.dot(a, b, preferred_element_type=F32)


def iota(shape, dim):
    return lax.broadcasted_iota(jnp.int32, shape, dim)


def kernel(
    sizes,
    ids_ref,
    gate_ref,
    adv_ref,
    lat_ref,
    noise_ref,
    shard_ref,
    fin_ref,
    nd_ref,
    meta_s,
    meta_r,
    gath,
    sel,
    selg,
    selgt,
    scale,
    send_a,
    send_b,
    recv_l,
    recv_n,
    recv_o,
    wbuf,
    perm,
    hid,
    hidp,
    term,
    gx,
    gsend,
    grecv,
    red_r,
    vel,
    meta_sem,
    gath_sem,
    l_sem,
    n_sem,
    o_sem,
    red_sem,
    wx_sem,
    wc_sem,
    gc_sem,
    gr_sem,
    dx_sem,
    dc_sem,
):
    images, n_role, n_dp, rate = sizes
    toks = lat_ref.shape[0]
    per_image = toks // images
    width = lat_ref.shape[1]
    half = width // 2
    hidden_units = wbuf.shape[1]
    rows = shard_ref.shape[1]
    slots = images * CAP
    blk = SIDE * slots
    total = SIDE * blk
    keep_gain, drift_gain, noise_gain = coefficients(0)

    role = lax.axis_index("role")
    ep = lax.axis_index("ep")
    dp = lax.axis_index("dp")
    z, y = lax.div(ep, SIDE), lax.rem(ep, SIDE)
    other = 1 - dp
    d1 = 1 - 2 * dp
    mine = role * n_dp + dp

    def pos_g(ax):
        return z * (1 - ax) + y * ax

    def pos_x(ax):
        return y * (1 - ax) + z * ax

    def dev_g(ax, i):
        return {"ep": (i * SIDE + y) * (1 - ax) + (z * SIDE + i) * ax}

    def dev_x(ax, i):
        return {"ep": (z * SIDE + i) * (1 - ax) + (i * SIDE + y) * ax}

    def ring(i):
        return lax.rem(i + 2 * SIDE, SIDE)

    def role_at(i):
        return lax.rem(role + n_role + i, n_role)

    def copy(src, dst, sems, at, dev):
        return pltpu.make_async_remote_copy(
            src_ref=src,
            dst_ref=dst,
            send_sem=sems.at[(0,) + at],
            recv_sem=sems.at[(1,) + at],
            device_id=dev,
            device_id_type=MESH,
        )

    def each(low, high, body):
        def step(i, carry):
            body(i)
            return carry

        lax.fori_loop(low, high, step, 0)

    def wrows(q):
        return pl.ds(pl.multiple_of(q * rows, rows), rows)

    def brows(i):
        return pl.ds(pl.multiple_of(i * blk, blk), blk)

    def trows(i):
        return pl.ds(pl.multiple_of(i * toks, toks), toks)

    barrier = pltpu.get_barrier_semaphore()

    def greet(j):
        for ax in (0, 1):
            pl.semaphore_signal(
                barrier, inc=1, device_id=dev_x(ax, ring(pos_x(ax) + j)), device_id_type=MESH
            )

    each(1, SIDE, greet)
    for i in range(1, n_role):
        pl.semaphore_signal(barrier, inc=1, device_id={"role": role_at(i)}, device_id_type=MESH)
    pl.semaphore_signal(barrier, inc=1, device_id={"dp": other}, device_id_type=MESH)

    for ax in (0, 1):
        cols = slice(ax * half, (ax + 1) * half)
        gath[0, ax, pos_g(ax)] = lat_ref[:, cols]
        gath[1, ax, pos_g(ax)] = noise_ref[:, cols]

    pl.semaphore_wait(barrier, 2 * (SIDE - 1) + n_role)

    def gath_hop(kind, ax, way, hop):
        step = d1 * (1 - 2 * way)
        slot = ring(pos_g(ax) - step * (hop - 1))
        block = gath.at[kind, ax, slot]
        return copy(block, block, gath_sem, (kind, ax, way, hop - 1), dev_g(ax, ring(pos_g(ax) + step)))

    def gath_wait(kind, ax, way, hop):
        step = d1 * (1 - 2 * way)
        block = gath.at[kind, ax, ring(pos_g(ax) - step * hop)]
        copy(block, block, gath_sem, (kind, ax, way, hop - 1), dev_g(ax, ring(pos_g(ax) + step))).wait_recv()

    def meta_copy(ax, j):
        return copy(
            meta_s.at[ax, ring(pos_g(ax) + j)],
            meta_r.at[ax, pos_g(ax)],
            meta_sem,
            (ax, j - 1),
            dev_g(ax, ring(pos_g(ax) + j)),
        )

    def meta_start(j):
        for ax in (0, 1):
            meta_copy(ax, j).start()

    for kind in (0, 1):
        for ax in (0, 1):
            for way in (0, 1):
                gath_hop(kind, ax, way, 1).start()

    def w_role(i):
        return copy(shard_ref, wbuf.at[:, wrows(mine), :], wx_sem, (i - 1,), {"role": role_at(i)})

    def w_core(i):
        q = role_at(-i) * n_dp + dp
        block = wbuf.at[:, wrows(q), :]
        return copy(block, block, wc_sem, (i,), {"dp": other})

    for i in range(1, n_role):
        w_role(i).start()

    row = iota((toks, toks), 0)
    lane = iota((toks, toks), 1)
    same = jnp.where(lane >= per_image, 1, 0) == jnp.where(row >= per_image, 1, 0)
    before = jnp.where(same & (row < lane), 1.0, 0.0).astype(BF16)
    experts = SIDE * SIDE
    expert_row = iota((experts, toks), 0)
    first_slot = jnp.where(iota((experts, toks), 1) >= per_image, float(CAP), 0.0)
    for ax in (0, 1):
        hit = jnp.zeros((experts, toks), F32)
        gate = jnp.zeros((experts, toks), F32)
        for k in range(ids_ref.shape[0]):
            named = jnp.concatenate([ids_ref[k, i : i + 1, :] for i in range(images)], axis=1)
            weight = jnp.concatenate([gate_ref[k, i : i + 1, :] for i in range(images)], axis=1)
            if ax == 1:
                named = (named & (SIDE - 1)) * SIDE + (named >> 3)
            at = named == expert_row
            hit = jnp.where(at, 1.0, hit)
            gate = jnp.where(at, weight, gate)
        place = jnp.where(hit > 0.5, mm(hit.astype(BF16), before) + first_slot, -1000.0)
        for i in range(SIDE):
            meta_s[ax, i, 0:SIDE, :] = place[i * SIDE : (i + 1) * SIDE]
            meta_s[ax, i, SIDE : 2 * SIDE, :] = gate[i * SIDE : (i + 1) * SIDE]
        meta_r[ax, pos_g(ax)] = meta_s[ax, pos_g(ax)]
    each(1, SIDE, meta_start)
    wbuf[:, wrows(mine), :] = shard_ref[...]
    w_core(0).start()

    def forward(kind, hop):
        for ax in (0, 1):
            for way in (0, 1):
                if hop <= 4 - way:
                    gath_wait(kind, ax, way, hop)
                    if hop + 1 <= 4 - way:
                        gath_hop(kind, ax, way, hop + 1).start()

    def meta_wait(j):
        for ax in (0, 1):
            slot = meta_r.at[ax, ring(pos_g(ax) - j)]
            copy(slot, slot, meta_sem, (ax, j - 1), dev_g(ax, ring(pos_g(ax) + j))).wait_recv()

    forward(0, 1)
    each(1, SIDE, meta_wait)
    gain = drift_gain / noise_gain
    lane1 = iota((1, toks), 1)
    factor = jnp.where(lane1 >= per_image, adv_ref[1] * gain, adv_ref[0] * gain)
    slot_row = iota((blk, toks), 0).astype(F32)

    def build(ax):
        def one(e):
            scaled = jnp.zeros((blk, 1), F32)
            for s in range(SIDE):
                place = meta_r[ax, s, pl.ds(e, 1), :]
                gate = meta_r[ax, s, pl.ds(SIDE + e, 1), :]
                at = (slot_row - float(slots * s)) == place
                cols = slice(s * toks, (s + 1) * toks)
                sel[ax, e, :, cols] = jnp.where(at, 1.0, 0.0).astype(BF16)
                selg[brows(e), cols] = jnp.where(at, gate, 0.0).astype(BF16)
                scaled = scaled + jnp.sum(jnp.where(at, gate * factor, 0.0), axis=1, keepdims=True)
            scale[ax, e] = jnp.broadcast_to(scaled, (blk, toks))

        each(0, SIDE, one)

        def turn(s):
            cols = pl.ds(pl.multiple_of(s * toks, toks), toks)
            for b in range(total // toks):
                part = selg[b * toks : (b + 1) * toks, cols].astype(F32)
                selgt[ax, s, :, b * toks : (b + 1) * toks] = part.T.astype(BF16)

        each(0, SIDE, turn)

    build(0)
    forward(1, 1)
    forward(0, 2)
    build(1)
    forward(1, 2)
    forward(0, 3)
    r_iota = iota((total, 1), 0)
    outer = lax.div(r_iota, blk)
    inner = lax.div(r_iota - outer * blk, slots)
    target = inner * blk + outer * slots + (r_iota - outer * blk - inner * slots)
    perm[...] = jnp.where(iota((total, total), 1) == target, 1.0, 0.0).astype(BF16)
    forward(1, 3)
    for i in range(1, n_role):
        q = role_at(-i) * n_dp + dp
        block = wbuf.at[:, wrows(q), :]
        copy(block, block, wx_sem, (i - 1,), {"role": role_at(i)}).wait_recv()
        w_core(i).start()
    forward(0, 4)

    everything = (0, half)

    def x_copy(buf, dst, sems, ax, j, pre=(), cols=everything):
        to = ring(pos_x(ax) + j)
        lanes = slice(*cols)
        return copy(
            buf.at[ax, brows(to), lanes], dst.at[ax, brows(pos_x(ax)), lanes], sems, pre + (ax, j - 1), dev_x(ax, to)
        )

    def x_wait(dst, sems, pre=(), cols=everything, low=1, high=SIDE):
        def one(j):
            for ax in (0, 1):
                block = dst.at[ax, brows(ring(pos_x(ax) - j)), slice(*cols)]
                copy(block, block, sems, pre + (ax, j - 1), dev_x(ax, ring(pos_x(ax) + j))).wait_recv()

        each(low, high, one)

    def x_sent(buf, dst, sems, pre=(), cols=everything):
        def one(j):
            for ax in (0, 1):
                x_copy(buf, dst, sems, ax, j, pre, cols).wait_send()

        each(1, SIDE, one)

    def far_first(body):
        def one(i):
            body(SIDE // 2 + (2 * lax.rem(i, 2) - 1) * lax.div(i, 2))

        each(1, SIDE, one)

    def picked(kind, ax, e):
        rows_ = gath[kind, ax].reshape(SIDE * toks, half)
        return mm(sel[ax, e], rows_)

    def pack_l(j):
        def one(ax):
            to = ring(pos_x(ax) + j)
            send_a[ax, brows(to), :] = picked(0, ax, to).astype(BF16)
            x_copy(send_a, recv_l, l_sem, ax, j).start()

        each(0, 2, one)

    far_first(pack_l)

    def own_l(ax):
        here = pos_x(ax)
        recv_l[ax, brows(here), :] = picked(0, ax, here).astype(BF16)

    each(0, 2, own_l)

    def pack_n(j):
        def one(ax):
            to = ring(pos_x(ax) + j)
            col = scale[ax, to][:, 0:1]
            send_b[ax, brows(to), :] = (col * picked(1, ax, to)).astype(BF16)

        each(0, 2, one)

    forward(1, 4)
    each(0, SIDE, pack_n)
    for ax in (0, 1):
        recv_n[ax, brows(pos_x(ax)), :] = send_b[ax, brows(pos_x(ax)), :]

    def start_n(j):
        for ax in (0, 1):
            x_copy(send_b, recv_n, n_sem, ax, j).start()

    far_first(start_n)
    x_wait(recv_l, l_sem)

    for i in range(n_role):
        q = role_at(-i) * n_dp + other
        block = wbuf.at[:, wrows(q), :]
        copy(block, block, wc_sem, (i,), {"dp": other}).wait_recv()
    x_sent(send_a, recv_l, l_sem)
    chunk = 256

    def cols_at(n):
        return pl.ds(pl.multiple_of(n * chunk, chunk), chunk)

    def align(n):
        send_a[1, :, cols_at(n)] = mm(perm[...], recv_l[1, :, cols_at(n)]).astype(BF16)

    each(0, half // chunk, align)

    def up(n):
        def nt(a, b):
            return lax.dot_general(a, b, (((1,), (1,)), ((), ())), preferred_element_type=F32)

        hrows = pl.ds(pl.multiple_of(n * chunk, chunk), chunk)
        pre = nt(recv_l[0], wbuf[0, hrows, 0:half]) + nt(send_a[1], wbuf[0, hrows, half:width])
        hidden = jax.nn.gelu(pre * (1.0 / math.sqrt(width)), approximate=True).astype(BF16)
        hid[:, cols_at(n)] = hidden
        hidp[:, cols_at(n)] = mm(perm[...], hidden).astype(BF16)

    each(0, hidden_units // chunk, up)
    down_gain = 1.0 / math.sqrt(hidden_units)

    parts = ((0, chunk), (chunk, 2 * chunk), (2 * chunk, half))

    for part, cols in enumerate(parts):
        for ax in (0, 1):
            source = hid if ax == 0 else hidp

            def down(n, ax=ax, source=source):
                lanes = pl.ds(pl.multiple_of(ax * half + n * chunk, chunk), chunk)
                send_a[ax, :, cols_at(n)] = (mm(source[...], wbuf[1, :, lanes]) * down_gain).astype(BF16)

            each(cols[0] // chunk, cols[1] // chunk, down)

            def start_o(j, ax=ax, part=part, cols=cols):
                x_copy(send_a, recv_o, o_sem, ax, j, (part,), cols).start()

            far_first(start_o)
    for ax in (0, 1):
        recv_o[ax, brows(pos_x(ax)), :] = send_a[ax, brows(pos_x(ax)), :]

    x_wait(recv_n, n_sem)
    for ax in (0, 1):
        source = hid if ax == 0 else hidp

        def outer_product(m, ax=ax, source=source):
            part = lax.dot_general(
                source[:, cols_at(m)], recv_n[ax], (((0,), (0,)), ((), ())), preferred_element_type=F32
            )
            mrows = pl.ds(pl.multiple_of(m * chunk, chunk), chunk)
            term[mrows, ax * half : (ax + 1) * half] = (part * down_gain).astype(BF16)

        each(0, hidden_units // chunk, outer_product)

    def g_core(i):
        return copy(term.at[wrows(i * n_dp + other), :], gx.at[i], gc_sem, (i,), {"dp": other})

    for i in range(n_role):
        g_core(i).start()

    def g_role(i):
        return copy(gsend.at[i - 1], grecv.at[i - 1], gr_sem, (i - 1,), {"role": role_at(i)})

    for i in range(n_role):
        copy(gx.at[i], gx.at[i], gc_sem, (i,), {"dp": other}).wait_recv()
    for i in range(1, n_role):
        to = role_at(i)
        gsend[i - 1] = (term[wrows(to * n_dp + dp), :].astype(F32) + gx[to].astype(F32)).astype(BF16)
        g_role(i).start()

    def weighed(part, ax, to):
        return mm(selgt[ax, to], recv_o[ax, :, slice(*parts[part])])

    def red_slot(way, k):
        return way * 4 + k - 1

    def red_copy(part, ax, way, k):
        step = d1 * (1 - 2 * way)
        slot = red_slot(way, k)
        lanes = slice(*parts[part])
        return copy(
            send_b.at[ax, trows(slot), lanes],
            red_r.at[ax, trows(slot), lanes],
            red_sem,
            (part, ax, slot),
            dev_g(ax, ring(pos_g(ax) + step)),
        )

    def red_arrived(part, ax, way, k):
        slot = red_slot(way, k)
        lanes = slice(*parts[part])
        block = red_r.at[ax, trows(slot), lanes]
        to = dev_g(ax, ring(pos_g(ax) + d1 * (1 - 2 * way)))
        copy(block, block, red_sem, (part, ax, slot), to).wait_recv()
        return red_r[ax, trows(slot), lanes].astype(F32)

    def prepare(part, k):
        def one(ax):
            for way in (0, 1):
                hops = 4 - way
                if k > hops and not (k == 5 and way == 0):
                    continue
                step = d1 * (1 - 2 * way)
                vel[ax, way, :, slice(*parts[part])] = weighed(part, ax, ring(pos_g(ax) + step * (hops + 1 - k)))

        each(0, 2, one)

    def push(part, k):
        lanes = slice(*parts[part])

        def one(ax):
            for way in (0, 1):
                if k > 4 - way:
                    continue
                value = vel[ax, way, :, lanes]
                if k > 1:
                    value = value + red_arrived(part, ax, way, k - 1)
                send_b[ax, trows(red_slot(way, k)), lanes] = value.astype(BF16)
                red_copy(part, ax, way, k).start()

        each(0, 2, one)
        prepare(part, k + 1)

    def finish(part):
        low, high = parts[part]
        for ax in (0, 1):
            cols = slice(ax * half + low, ax * half + high)
            velocity = vel[ax, 0, :, low:high] + red_arrived(part, ax, 1, 3) + red_arrived(part, ax, 0, 4)
            moved = (
                keep_gain * lat_ref[:, cols].astype(F32)
                + drift_gain * velocity
                + noise_gain * noise_ref[:, cols].astype(F32)
            )
            fin_ref[:, cols] = moved.astype(BF16)

    x_wait(recv_o, o_sem, (0,), parts[0])
    x_sent(send_b, recv_n, n_sem)
    prepare(0, 1)
    push(0, 1)
    push(0, 2)

    for i in range(1, n_role):
        copy(grecv.at[i - 1], grecv.at[i - 1], gr_sem, (i - 1,), {"role": role_at(i)}).wait_recv()
    grad = term[wrows(mine), :].astype(F32) + gx[role].astype(F32)
    for i in range(1, n_role):
        grad = grad + grecv[i - 1].astype(F32)
    nd_ref[wrows(mine), :] = (wbuf[1, wrows(mine), :].astype(F32) + rate * grad).astype(BF16)

    def d_role(i):
        block = nd_ref.at[wrows(mine), :]
        return copy(block, block, dx_sem, (i - 1,), {"role": role_at(i)})

    def d_core(i):
        block = nd_ref.at[wrows(role_at(-i) * n_dp + dp), :]
        return copy(block, block, dc_sem, (i,), {"dp": other})

    for i in range(1, n_role):
        d_role(i).start()
    d_core(0).start()

    x_wait(recv_o, o_sem, (1,), parts[1])
    prepare(1, 1)
    push(1, 1)
    push(0, 3)
    x_wait(recv_o, o_sem, (2,), parts[2])
    prepare(2, 1)
    push(2, 1)
    push(1, 2)
    push(0, 4)
    push(2, 2)
    push(1, 3)

    for i in range(1, n_role):
        block = nd_ref.at[wrows(role_at(-i) * n_dp + dp), :]
        copy(block, block, dx_sem, (i - 1,), {"role": role_at(i)}).wait_recv()
        d_core(i).start()

    push(2, 3)
    push(1, 4)
    finish(0)
    push(2, 4)
    finish(1)
    finish(2)

    for i in range(n_role):
        block = nd_ref.at[wrows(role_at(-i) * n_dp + other), :]
        copy(block, block, dc_sem, (i,), {"dp": other}).wait_recv()

    def meta_sent(j):
        for ax in (0, 1):
            meta_copy(ax, j).wait_send()

    each(1, SIDE, meta_sent)
    for kind in (0, 1):
        for ax in (0, 1):
            for way in (0, 1):
                for hop in range(1, 5 - way):
                    gath_hop(kind, ax, way, hop).wait_send()
    for part, cols in enumerate(parts):
        x_sent(send_a, recv_o, o_sem, (part,), cols)
    for part in range(len(parts)):
        for ax in (0, 1):
            for way in (0, 1):
                for k in range(1, 5 - way):
                    red_copy(part, ax, way, k).wait_send()
    for i in range(1, n_role):
        w_role(i).wait_send()
        g_role(i).wait_send()
        d_role(i).wait_send()
    for i in range(n_role):
        w_core(i).wait_send()
        g_core(i).wait_send()
        d_core(i).wait_send()


def per_device(latents, noise, expert_ids, gate_values, advantages, expert_pair):
    n_role, n_dp, n_ep = lax.axis_size("role"), lax.axis_size("dp"), lax.axis_size("ep")
    images, tok_count, width = latents.shape
    top = expert_ids.shape[3]
    toks = images * tok_count
    rows = expert_pair.shape[2]
    hidden_units = rows * n_role * n_dp
    experts = expert_pair.shape[0] * n_ep
    half = width // 2
    slots = images * CAP
    blk = SIDE * slots
    total = SIDE * blk
    rate = 10.0 / math.sqrt(tok_count * n_ep * top * images * n_role * n_dp / experts)
    vmem = pl.BlockSpec(memory_space=pltpu.VMEM)
    dma = pltpu.SemaphoreType.DMA
    fin, new_down = pl.pallas_call(
        functools.partial(kernel, (images, n_role, n_dp, rate)),
        out_shape=(
            pltpu.VMEM((toks, width), BF16),
            pltpu.VMEM((hidden_units, width), BF16),
        ),
        in_specs=[vmem, vmem, pl.BlockSpec(memory_space=pltpu.SMEM), vmem, vmem, vmem],
        out_specs=(vmem, vmem),
        scratch_shapes=[
            pltpu.VMEM((2, SIDE, 2 * SIDE, toks), F32),
            pltpu.VMEM((2, SIDE, 2 * SIDE, toks), F32),
            pltpu.VMEM((2, 2, SIDE, toks, half), BF16),
            pltpu.VMEM((2, SIDE, blk, SIDE * toks), BF16),
            pltpu.VMEM((total, SIDE * toks), BF16),
            pltpu.VMEM((2, SIDE, toks, total), BF16),
            pltpu.VMEM((2, SIDE, blk, toks), F32),
            pltpu.VMEM((2, total, half), BF16),
            pltpu.VMEM((2, total, half), BF16),
            pltpu.VMEM((2, total, half), BF16),
            pltpu.VMEM((2, total, half), BF16),
            pltpu.VMEM((2, total, half), BF16),
            pltpu.VMEM((2, hidden_units, width), BF16),
            pltpu.VMEM((total, total), BF16),
            pltpu.VMEM((total, hidden_units), BF16),
            pltpu.VMEM((total, hidden_units), BF16),
            pltpu.VMEM((hidden_units, width), BF16),
            pltpu.VMEM((n_role, rows, width), BF16),
            pltpu.VMEM((n_role - 1, rows, width), BF16),
            pltpu.VMEM((n_role - 1, rows, width), BF16),
            pltpu.VMEM((2, 7 * toks, half), BF16),
            pltpu.VMEM((2, 2, toks, half), F32),
            dma((2, 2, SIDE - 1)),
            dma((2, 2, 2, 2, 4)),
            dma((2, 2, SIDE - 1)),
            dma((2, 2, SIDE - 1)),
            dma((2, 3, 2, SIDE - 1)),
            dma((2, 3, 2, 7)),
            dma((2, n_role - 1)),
            dma((2, n_role)),
            dma((2, n_role)),
            dma((2, n_role - 1)),
            dma((2, n_role - 1)),
            dma((2, n_role)),
        ],
        compiler_params=pltpu.CompilerParams(
            collective_id=0, has_side_effects=True, vmem_limit_bytes=56 * 1024 * 1024
        ),
    )(
        jnp.transpose(expert_ids[0], (2, 0, 1)),
        jnp.transpose(gate_values[0], (2, 0, 1)),
        advantages,
        latents.reshape(toks, width),
        noise.reshape(toks, width),
        expert_pair.reshape(2, rows, width),
    )
    return (fin.reshape(images, tok_count, width), new_down.reshape(1, hidden_units, width))


def solution(mesh):
    in_specs = (
        P(("role", "dp"), "ep", None),
        P(None, ("role", "dp"), "ep", None),
        P(None, ("role", "dp"), "ep", None),
        P(None, ("role", "dp"), "ep", None),
        P(("role", "dp")),
        P("ep", None, ("role", "dp"), None),
    )
    out_specs = (P(("role", "dp"), "ep", None), P("ep", None, None))
    return jax.shard_map(
        per_device, mesh=mesh, in_specs=in_specs, out_specs=out_specs, check_vma=False
    )
```

```python
import functools
import math

import jax
import jax.numpy as jnp
from jax import lax
from jax.experimental import pallas as pl
from jax.experimental.pallas import tpu as pltpu
from jax.sharding import PartitionSpec as P

CAP = 7
SIDE = 8
MESH = pl.DeviceIdType.MESH
F32 = jnp.float32
BF16 = jnp.bfloat16


def coefficients(section):
    moment = 0.95 - 0.4 * section
    noise_level = 0.3 * math.sqrt(moment / (1.0 - moment))
    factor = noise_level * noise_level / (2.0 * moment)
    keep_gain = 1.0 - 0.4 * factor
    drift_gain = -0.4 * (1.0 + factor * (1.0 - moment))
    noise_gain = noise_level * math.sqrt(0.4)
    return (keep_gain, drift_gain, noise_gain)


def mm(a, b):
    return jnp.dot(a, b, preferred_element_type=F32)


def iota(shape, dim):
    return lax.broadcasted_iota(jnp.int32, shape, dim)


def kernel(
    sizes,
    ids_ref,
    gate_ref,
    adv_ref,
    lat_ref,
    noise_ref,
    shard_ref,
    fin_ref,
    nd_ref,
    meta_s,
    meta_r,
    gath,
    sel,
    selg,
    selgt,
    scale,
    send_a,
    send_b,
    recv_l,
    recv_n,
    recv_o,
    wbuf,
    perm,
    hid,
    hidp,
    term,
    gx,
    gsend,
    grecv,
    red_r,
    vel,
    meta_sem,
    gath_sem,
    l_sem,
    n_sem,
    o_sem,
    red_sem,
    wx_sem,
    wc_sem,
    gc_sem,
    gr_sem,
    dx_sem,
    dc_sem,
):
    images, n_role, n_dp, rate = sizes
    toks = lat_ref.shape[0]
    per_image = toks // images
    width = lat_ref.shape[1]
    half = width // 2
    hidden_units = wbuf.shape[1]
    rows = shard_ref.shape[1]
    slots = images * CAP
    blk = SIDE * slots
    total = SIDE * blk
    keep_gain, drift_gain, noise_gain = coefficients(0)

    role = lax.axis_index("role")
    ep = lax.axis_index("ep")
    dp = lax.axis_index("dp")
    z, y = lax.div(ep, SIDE), lax.rem(ep, SIDE)
    other = 1 - dp
    d1 = 1 - 2 * dp
    mine = role * n_dp + dp

    def pos_g(ax):
        return z * (1 - ax) + y * ax

    def pos_x(ax):
        return y * (1 - ax) + z * ax

    def dev_g(ax, i):
        return {"ep": (i * SIDE + y) * (1 - ax) + (z * SIDE + i) * ax}

    def dev_x(ax, i):
        return {"ep": (z * SIDE + i) * (1 - ax) + (i * SIDE + y) * ax}

    def ring(i):
        return lax.rem(i + 2 * SIDE, SIDE)

    def role_at(i):
        return lax.rem(role + n_role + i, n_role)

    def copy(src, dst, sems, at, dev):
        return pltpu.make_async_remote_copy(
            src_ref=src,
            dst_ref=dst,
            send_sem=sems.at[(0,) + at],
            recv_sem=sems.at[(1,) + at],
            device_id=dev,
            device_id_type=MESH,
        )

    def each(low, high, body):
        def step(i, carry):
            body(i)
            return carry

        lax.fori_loop(low, high, step, 0)

    def wrows(q):
        return pl.ds(pl.multiple_of(q * rows, rows), rows)

    def brows(i):
        return pl.ds(pl.multiple_of(i * blk, blk), blk)

    def trows(i):
        return pl.ds(pl.multiple_of(i * toks, toks), toks)

    barrier = pltpu.get_barrier_semaphore()

    def greet(j):
        for ax in (0, 1):
            pl.semaphore_signal(
                barrier, inc=1, device_id=dev_x(ax, ring(pos_x(ax) + j)), device_id_type=MESH
            )

    each(1, SIDE, greet)
    for i in range(1, n_role):
        pl.semaphore_signal(barrier, inc=1, device_id={"role": role_at(i)}, device_id_type=MESH)
    pl.semaphore_signal(barrier, inc=1, device_id={"dp": other}, device_id_type=MESH)

    for ax in (0, 1):
        cols = slice(ax * half, (ax + 1) * half)
        gath[0, ax, pos_g(ax)] = lat_ref[:, cols]
        gath[1, ax, pos_g(ax)] = noise_ref[:, cols]

    pl.semaphore_wait(barrier, 2 * (SIDE - 1) + n_role)

    def gath_hop(kind, ax, way, hop):
        step = d1 * (1 - 2 * way)
        slot = ring(pos_g(ax) - step * (hop - 1))
        block = gath.at[kind, ax, slot]
        return copy(block, block, gath_sem, (kind, ax, way, hop - 1), dev_g(ax, ring(pos_g(ax) + step)))

    def gath_wait(kind, ax, way, hop):
        step = d1 * (1 - 2 * way)
        block = gath.at[kind, ax, ring(pos_g(ax) - step * hop)]
        copy(block, block, gath_sem, (kind, ax, way, hop - 1), dev_g(ax, ring(pos_g(ax) + step))).wait_recv()

    def meta_copy(ax, j):
        return copy(
            meta_s.at[ax, ring(pos_g(ax) + j)],
            meta_r.at[ax, pos_g(ax)],
            meta_sem,
            (ax, j - 1),
            dev_g(ax, ring(pos_g(ax) + j)),
        )

    def meta_start(j):
        for ax in (0, 1):
            meta_copy(ax, j).start()

    for kind in (0, 1):
        for ax in (0, 1):
            for way in (0, 1):
                gath_hop(kind, ax, way, 1).start()

    def w_role(i):
        return copy(shard_ref, wbuf.at[:, wrows(mine), :], wx_sem, (i - 1,), {"role": role_at(i)})

    def w_core(i):
        q = role_at(-i) * n_dp + dp
        block = wbuf.at[:, wrows(q), :]
        return copy(block, block, wc_sem, (i,), {"dp": other})

    for i in range(1, n_role):
        w_role(i).start()

    row = iota((toks, toks), 0)
    lane = iota((toks, toks), 1)
    same = jnp.where(lane >= per_image, 1, 0) == jnp.where(row >= per_image, 1, 0)
    before = jnp.where(same & (row < lane), 1.0, 0.0).astype(BF16)
    experts = SIDE * SIDE
    expert_row = iota((experts, toks), 0)
    first_slot = jnp.where(iota((experts, toks), 1) >= per_image, float(CAP), 0.0)
    for ax in (0, 1):
        hit = jnp.zeros((experts, toks), F32)
        gate = jnp.zeros((experts, toks), F32)
        for k in range(ids_ref.shape[0]):
            named = jnp.concatenate([ids_ref[k, i : i + 1, :] for i in range(images)], axis=1)
            weight = jnp.concatenate([gate_ref[k, i : i + 1, :] for i in range(images)], axis=1)
            if ax == 1:
                named = (named & (SIDE - 1)) * SIDE + (named >> 3)
            at = named == expert_row
            hit = jnp.where(at, 1.0, hit)
            gate = jnp.where(at, weight, gate)
        place = jnp.where(hit > 0.5, mm(hit.astype(BF16), before) + first_slot, -1000.0)
        for i in range(SIDE):
            meta_s[ax, i, 0:SIDE, :] = place[i * SIDE : (i + 1) * SIDE]
            meta_s[ax, i, SIDE : 2 * SIDE, :] = gate[i * SIDE : (i + 1) * SIDE]
        meta_r[ax, pos_g(ax)] = meta_s[ax, pos_g(ax)]
    each(1, SIDE, meta_start)
    wbuf[:, wrows(mine), :] = shard_ref[...]
    w_core(0).start()

    def forward(kind, hop):
        for ax in (0, 1):
            for way in (0, 1):
                if hop <= 4 - way:
                    gath_wait(kind, ax, way, hop)
                    if hop + 1 <= 4 - way:
                        gath_hop(kind, ax, way, hop + 1).start()

    def meta_wait(j):
        for ax in (0, 1):
            slot = meta_r.at[ax, ring(pos_g(ax) - j)]
            copy(slot, slot, meta_sem, (ax, j - 1), dev_g(ax, ring(pos_g(ax) + j))).wait_recv()

    forward(0, 1)
    each(1, SIDE, meta_wait)
    gain = drift_gain / noise_gain
    lane1 = iota((1, toks), 1)
    factor = jnp.where(lane1 >= per_image, adv_ref[1] * gain, adv_ref[0] * gain)
    slot_row = iota((blk, toks), 0).astype(F32)

    def build(ax):
        def one(e):
            scaled = jnp.zeros((blk, 1), F32)
            for s in range(SIDE):
                place = meta_r[ax, s, pl.ds(e, 1), :]
                gate = meta_r[ax, s, pl.ds(SIDE + e, 1), :]
                at = (slot_row - float(slots * s)) == place
                cols = slice(s * toks, (s + 1) * toks)
                sel[ax, e, :, cols] = jnp.where(at, 1.0, 0.0).astype(BF16)
                selg[brows(e), cols] = jnp.where(at, gate, 0.0).astype(BF16)
                scaled = scaled + jnp.sum(jnp.where(at, gate * factor, 0.0), axis=1, keepdims=True)
            scale[ax, e] = jnp.broadcast_to(scaled, (blk, toks))

        each(0, SIDE, one)

        def turn(s):
            cols = pl.ds(pl.multiple_of(s * toks, toks), toks)
            for b in range(total // toks):
                part = selg[b * toks : (b + 1) * toks, cols].astype(F32)
                selgt[ax, s, :, b * toks : (b + 1) * toks] = part.T.astype(BF16)

        each(0, SIDE, turn)

    build(0)
    forward(1, 1)
    forward(0, 2)
    build(1)
    forward(1, 2)
    forward(0, 3)
    r_iota = iota((total, 1), 0)
    outer = lax.div(r_iota, blk)
    inner = lax.div(r_iota - outer * blk, slots)
    target = inner * blk + outer * slots + (r_iota - outer * blk - inner * slots)
    perm[...] = jnp.where(iota((total, total), 1) == target, 1.0, 0.0).astype(BF16)
    forward(1, 3)
    for i in range(1, n_role):
        q = role_at(-i) * n_dp + dp
        block = wbuf.at[:, wrows(q), :]
        copy(block, block, wx_sem, (i - 1,), {"role": role_at(i)}).wait_recv()
        w_core(i).start()
    forward(0, 4)

    everything = (0, half)

    def x_copy(buf, dst, sems, ax, j, pre=(), cols=everything):
        to = ring(pos_x(ax) + j)
        lanes = slice(*cols)
        return copy(
            buf.at[ax, brows(to), lanes], dst.at[ax, brows(pos_x(ax)), lanes], sems, pre + (ax, j - 1), dev_x(ax, to)
        )

    def x_wait(dst, sems, pre=(), cols=everything, low=1, high=SIDE):
        def one(j):
            for ax in (0, 1):
                block = dst.at[ax, brows(ring(pos_x(ax) - j)), slice(*cols)]
                copy(block, block, sems, pre + (ax, j - 1), dev_x(ax, ring(pos_x(ax) + j))).wait_recv()

        each(low, high, one)

    def x_sent(buf, dst, sems, pre=(), cols=everything):
        def one(j):
            for ax in (0, 1):
                x_copy(buf, dst, sems, ax, j, pre, cols).wait_send()

        each(1, SIDE, one)

    def far_first(body):
        def one(i):
            body(SIDE // 2 + (2 * lax.rem(i, 2) - 1) * lax.div(i, 2))

        each(1, SIDE, one)

    def picked(kind, ax, e):
        rows_ = gath[kind, ax].reshape(SIDE * toks, half)
        return mm(sel[ax, e], rows_)

    def pack_l(j):
        def one(ax):
            to = ring(pos_x(ax) + j)
            send_a[ax, brows(to), :] = picked(0, ax, to).astype(BF16)
            x_copy(send_a, recv_l, l_sem, ax, j).start()

        each(0, 2, one)

    far_first(pack_l)

    def own_l(ax):
        here = pos_x(ax)
        recv_l[ax, brows(here), :] = picked(0, ax, here).astype(BF16)

    each(0, 2, own_l)

    def pack_n(j):
        def one(ax):
            to = ring(pos_x(ax) + j)
            col = scale[ax, to][:, 0:1]
            send_b[ax, brows(to), :] = (col * picked(1, ax, to)).astype(BF16)

        each(0, 2, one)

    forward(1, 4)
    each(0, SIDE, pack_n)
    for ax in (0, 1):
        recv_n[ax, brows(pos_x(ax)), :] = send_b[ax, brows(pos_x(ax)), :]

    def start_n(j):
        for ax in (0, 1):
            x_copy(send_b, recv_n, n_sem, ax, j).start()

    far_first(start_n)
    x_wait(recv_l, l_sem)

    for i in range(n_role):
        q = role_at(-i) * n_dp + other
        block = wbuf.at[:, wrows(q), :]
        copy(block, block, wc_sem, (i,), {"dp": other}).wait_recv()
    x_sent(send_a, recv_l, l_sem)
    chunk = 256

    def cols_at(n):
        return pl.ds(pl.multiple_of(n * chunk, chunk), chunk)

    def align(n):
        send_a[1, :, cols_at(n)] = mm(perm[...], recv_l[1, :, cols_at(n)]).astype(BF16)

    each(0, half // chunk, align)

    def up(n):
        def nt(a, b):
            return lax.dot_general(a, b, (((1,), (1,)), ((), ())), preferred_element_type=F32)

        hrows = pl.ds(pl.multiple_of(n * chunk, chunk), chunk)
        pre = nt(recv_l[0], wbuf[0, hrows, 0:half]) + nt(send_a[1], wbuf[0, hrows, half:width])
        hidden = jax.nn.gelu(pre * (1.0 / math.sqrt(width)), approximate=True).astype(BF16)
        hid[:, cols_at(n)] = hidden
        hidp[:, cols_at(n)] = mm(perm[...], hidden).astype(BF16)

    each(0, hidden_units // chunk, up)
    down_gain = 1.0 / math.sqrt(hidden_units)

    parts = ((0, chunk), (chunk, 2 * chunk), (2 * chunk, half))

    for part, cols in enumerate(parts):
        for ax in (0, 1):
            source = hid if ax == 0 else hidp

            def down(n, ax=ax, source=source):
                lanes = pl.ds(pl.multiple_of(ax * half + n * chunk, chunk), chunk)
                send_a[ax, :, cols_at(n)] = (mm(source[...], wbuf[1, :, lanes]) * down_gain).astype(BF16)

            each(cols[0] // chunk, cols[1] // chunk, down)

            def start_o(j, ax=ax, part=part, cols=cols):
                x_copy(send_a, recv_o, o_sem, ax, j, (part,), cols).start()

            far_first(start_o)
    for ax in (0, 1):
        recv_o[ax, brows(pos_x(ax)), :] = send_a[ax, brows(pos_x(ax)), :]

    x_wait(recv_n, n_sem)
    for ax in (0, 1):
        source = hid if ax == 0 else hidp

        def outer_product(m, ax=ax, source=source):
            part = lax.dot_general(
                source[:, cols_at(m)], recv_n[ax], (((0,), (0,)), ((), ())), preferred_element_type=F32
            )
            mrows = pl.ds(pl.multiple_of(m * chunk, chunk), chunk)
            term[mrows, ax * half : (ax + 1) * half] = (part * down_gain).astype(BF16)

        each(0, hidden_units // chunk, outer_product)

    def g_core(i):
        return copy(term.at[wrows(i * n_dp + other), :], gx.at[i], gc_sem, (i,), {"dp": other})

    for i in range(n_role):
        g_core(i).start()

    def g_role(i):
        return copy(gsend.at[i - 1], grecv.at[i - 1], gr_sem, (i - 1,), {"role": role_at(i)})

    for i in range(n_role):
        copy(gx.at[i], gx.at[i], gc_sem, (i,), {"dp": other}).wait_recv()
    for i in range(1, n_role):
        to = role_at(i)
        gsend[i - 1] = (term[wrows(to * n_dp + dp), :].astype(F32) + gx[to].astype(F32)).astype(BF16)
        g_role(i).start()

    def weighed(part, ax, to):
        return mm(selgt[ax, to], recv_o[ax, :, slice(*parts[part])])

    def red_slot(way, k):
        return way * 4 + k - 1

    def red_copy(part, ax, way, k):
        step = d1 * (1 - 2 * way)
        slot = red_slot(way, k)
        lanes = slice(*parts[part])
        return copy(
            send_b.at[ax, trows(slot), lanes],
            red_r.at[ax, trows(slot), lanes],
            red_sem,
            (part, ax, slot),
            dev_g(ax, ring(pos_g(ax) + step)),
        )

    def red_arrived(part, ax, way, k):
        slot = red_slot(way, k)
        lanes = slice(*parts[part])
        block = red_r.at[ax, trows(slot), lanes]
        to = dev_g(ax, ring(pos_g(ax) + d1 * (1 - 2 * way)))
        copy(block, block, red_sem, (part, ax, slot), to).wait_recv()
        return red_r[ax, trows(slot), lanes].astype(F32)

    def prepare(part, k):
        def one(ax):
            for way in (0, 1):
                hops = 4 - way
                if k > hops and not (k == 5 and way == 0):
                    continue
                step = d1 * (1 - 2 * way)
                vel[ax, way, :, slice(*parts[part])] = weighed(part, ax, ring(pos_g(ax) + step * (hops + 1 - k)))

        each(0, 2, one)

    def push(part, k):
        lanes = slice(*parts[part])

        def one(ax):
            for way in (0, 1):
                if k > 4 - way:
                    continue
                value = vel[ax, way, :, lanes]
                if k > 1:
                    value = value + red_arrived(part, ax, way, k - 1)
                send_b[ax, trows(red_slot(way, k)), lanes] = value.astype(BF16)
                red_copy(part, ax, way, k).start()

        each(0, 2, one)
        prepare(part, k + 1)

    def finish(part):
        low, high = parts[part]
        for ax in (0, 1):
            cols = slice(ax * half + low, ax * half + high)
            velocity = vel[ax, 0, :, low:high] + red_arrived(part, ax, 1, 3) + red_arrived(part, ax, 0, 4)
            moved = (
                keep_gain * lat_ref[:, cols].astype(F32)
                + drift_gain * velocity
                + noise_gain * noise_ref[:, cols].astype(F32)
            )
            fin_ref[:, cols] = moved.astype(BF16)

    def meta_sent(j):
        for ax in (0, 1):
            meta_copy(ax, j).wait_send()

    each(1, SIDE, meta_sent)
    for kind in (0, 1):
        for ax in (0, 1):
            for way in (0, 1):
                for hop in range(1, 5 - way):
                    gath_hop(kind, ax, way, hop).wait_send()
    for i in range(1, n_role):
        w_role(i).wait_send()
    for i in range(n_role):
        w_core(i).wait_send()
        g_core(i).wait_send()

    def reduced(part):
        for ax in (0, 1):
            for way in (0, 1):
                for k in range(1, 5 - way):
                    red_copy(part, ax, way, k).wait_send()

    x_wait(recv_o, o_sem, (0,), parts[0])
    x_sent(send_b, recv_n, n_sem)
    prepare(0, 1)
    push(0, 1)
    push(0, 2)

    for i in range(1, n_role):
        copy(grecv.at[i - 1], grecv.at[i - 1], gr_sem, (i - 1,), {"role": role_at(i)}).wait_recv()
    grad = term[wrows(mine), :].astype(F32) + gx[role].astype(F32)
    for i in range(1, n_role):
        grad = grad + grecv[i - 1].astype(F32)
    nd_ref[wrows(mine), :] = (wbuf[1, wrows(mine), :].astype(F32) + rate * grad).astype(BF16)

    def d_role(i):
        block = nd_ref.at[wrows(mine), :]
        return copy(block, block, dx_sem, (i - 1,), {"role": role_at(i)})

    def d_core(i):
        block = nd_ref.at[wrows(role_at(-i) * n_dp + dp), :]
        return copy(block, block, dc_sem, (i,), {"dp": other})

    for i in range(1, n_role):
        d_role(i).start()
    d_core(0).start()

    x_wait(recv_o, o_sem, (1,), parts[1])
    prepare(1, 1)
    push(1, 1)
    push(0, 3)
    x_wait(recv_o, o_sem, (2,), parts[2])
    prepare(2, 1)
    push(2, 1)
    push(1, 2)
    push(0, 4)
    push(2, 2)
    push(1, 3)

    for i in range(1, n_role):
        block = nd_ref.at[wrows(role_at(-i) * n_dp + dp), :]
        copy(block, block, dx_sem, (i - 1,), {"role": role_at(i)}).wait_recv()
        d_core(i).start()

    push(2, 3)
    push(1, 4)
    finish(0)
    push(2, 4)
    for part, cols in enumerate(parts):
        x_sent(send_a, recv_o, o_sem, (part,), cols)
    for i in range(1, n_role):
        g_role(i).wait_send()
    reduced(0)
    reduced(1)
    finish(1)
    finish(2)

    for i in range(n_role):
        block = nd_ref.at[wrows(role_at(-i) * n_dp + other), :]
        copy(block, block, dc_sem, (i,), {"dp": other}).wait_recv()

    reduced(2)
    for i in range(1, n_role):
        d_role(i).wait_send()
    for i in range(n_role):
        d_core(i).wait_send()


def per_device(latents, noise, expert_ids, gate_values, advantages, expert_pair):
    n_role, n_dp, n_ep = lax.axis_size("role"), lax.axis_size("dp"), lax.axis_size("ep")
    images, tok_count, width = latents.shape
    top = expert_ids.shape[3]
    toks = images * tok_count
    rows = expert_pair.shape[2]
    hidden_units = rows * n_role * n_dp
    experts = expert_pair.shape[0] * n_ep
    half = width // 2
    slots = images * CAP
    blk = SIDE * slots
    total = SIDE * blk
    rate = 10.0 / math.sqrt(tok_count * n_ep * top * images * n_role * n_dp / experts)
    vmem = pl.BlockSpec(memory_space=pltpu.VMEM)
    dma = pltpu.SemaphoreType.DMA
    fin, new_down = pl.pallas_call(
        functools.partial(kernel, (images, n_role, n_dp, rate)),
        out_shape=(
            pltpu.VMEM((toks, width), BF16),
            pltpu.VMEM((hidden_units, width), BF16),
        ),
        in_specs=[vmem, vmem, pl.BlockSpec(memory_space=pltpu.SMEM), vmem, vmem, vmem],
        out_specs=(vmem, vmem),
        scratch_shapes=[
            pltpu.VMEM((2, SIDE, 2 * SIDE, toks), F32),
            pltpu.VMEM((2, SIDE, 2 * SIDE, toks), F32),
            pltpu.VMEM((2, 2, SIDE, toks, half), BF16),
            pltpu.VMEM((2, SIDE, blk, SIDE * toks), BF16),
            pltpu.VMEM((total, SIDE * toks), BF16),
            pltpu.VMEM((2, SIDE, toks, total), BF16),
            pltpu.VMEM((2, SIDE, blk, toks), F32),
            pltpu.VMEM((2, total, half), BF16),
            pltpu.VMEM((2, total, half), BF16),
            pltpu.VMEM((2, total, half), BF16),
            pltpu.VMEM((2, total, half), BF16),
            pltpu.VMEM((2, total, half), BF16),
            pltpu.VMEM((2, hidden_units, width), BF16),
            pltpu.VMEM((total, total), BF16),
            pltpu.VMEM((total, hidden_units), BF16),
            pltpu.VMEM((total, hidden_units), BF16),
            pltpu.VMEM((hidden_units, width), BF16),
            pltpu.VMEM((n_role, rows, width), BF16),
            pltpu.VMEM((n_role - 1, rows, width), BF16),
            pltpu.VMEM((n_role - 1, rows, width), BF16),
            pltpu.VMEM((2, 7 * toks, half), BF16),
            pltpu.VMEM((2, 2, toks, half), F32),
            dma((2, 2, SIDE - 1)),
            dma((2, 2, 2, 2, 4)),
            dma((2, 2, SIDE - 1)),
            dma((2, 2, SIDE - 1)),
            dma((2, 3, 2, SIDE - 1)),
            dma((2, 3, 2, 7)),
            dma((2, n_role - 1)),
            dma((2, n_role)),
            dma((2, n_role)),
            dma((2, n_role - 1)),
            dma((2, n_role - 1)),
            dma((2, n_role)),
        ],
        compiler_params=pltpu.CompilerParams(
            collective_id=0, has_side_effects=True, vmem_limit_bytes=56 * 1024 * 1024
        ),
    )(
        jnp.transpose(expert_ids[0], (2, 0, 1)),
        jnp.transpose(gate_values[0], (2, 0, 1)),
        advantages,
        latents.reshape(toks, width),
        noise.reshape(toks, width),
        expert_pair.reshape(2, rows, width),
    )
    return (fin.reshape(images, tok_count, width), new_down.reshape(1, hidden_units, width))


def solution(mesh):
    in_specs = (
        P(("role", "dp"), "ep", None),
        P(None, ("role", "dp"), "ep", None),
        P(None, ("role", "dp"), "ep", None),
        P(None, ("role", "dp"), "ep", None),
        P(("role", "dp")),
        P("ep", None, ("role", "dp"), None),
    )
    out_specs = (P(("role", "dp"), "ep", None), P("ep", None, None))
    return jax.shard_map(
        per_device, mesh=mesh, in_specs=in_specs, out_specs=out_specs, check_vma=False
    )
```
